512 devices in a mesh: ctx: 32 (over y, x), dp: 16 (over z, core).
Axes of the slice: x: 4, y: 8, z: 8, core: 2. Of those that a mesh axis runs over, the one named last changes fastest.
Arguments:
- queries: bfloat16 [32, 16, 2304, 128], P('dp', None, 'ctx'), may hold values from -6 to 6
- keys: bfloat16 [32, 16, 2304, 128], P('dp', None, 'ctx'), may hold values from -6 to 6
- values: bfloat16 [32, 16, 2304, 128], P('dp', None, 'ctx'), may hold values from -6 to 6
- out_grad: bfloat16 [32, 16, 2304, 128], P('dp', None, 'ctx'), may hold values from -6 to 6
- gains: float32 [2, 128], replicated, may hold values from 0.5 to 8, as said below
- keep_order: int32 [32, 32, 72], P('dp'), may hold values from 0 to 71, each once within a row
- keep_count: int32 [32, 32], P('dp'), may hold values from 1 to 54, 1152 in all within a row
Outputs:
- attn_out: bfloat16 [32, 16, 2304, 128], P('dp', None, 'ctx')
- query_grad: bfloat16 [32, 16, 2304, 128], P('dp', None, 'ctx')
- key_grad: bfloat16 [32, 16, 2304, 128], P('dp', None, 'ctx')
- value_grad: bfloat16 [32, 16, 2304, 128], P('dp', None, 'ctx')
- gain_grad: float32 [2, 128], replicated
The draws below stay inside these ranges and needn't reach their ends.
Inputs may be any that keep to these rules, and one draw needn't show every extreme that they name: `keep_order`: each row lists the 72 positions of one shard once; its first keep_count entries are that shard's kept tokens, in rank order. `keep_count`: for each sample the counts sum to 1152; some shard of every sample holds exactly 54. `gains`: Positive.
All inputs are finite; a program needn't handle non-finite values.
Results may differ from the reference program's by a relative error of at most 0.017.
The reference program's roundings to bfloat16 on the way count: a program that leaves them out, or rounds other values in their place, can miss the bound.
Values may be sent and summed in bfloat16 or wider, within the bound.
A program may use at most 64 MiB of HBM per device.

```python
import math
import jax
import jax.numpy as jnp
import numpy as np
from jax import lax

HEADS = 16
HEAD_DIM = 128
TS = 72
MOST = 54
SEQ_LEN = 2304
KEPT = 1152
BATCH = 32
N_CTX = 32


def shared_normal(key):
    return jax.random.normal(key, (BATCH, HEADS, SEQ_LEN, HEAD_DIM), jnp.float32)


def draw_queries(key, part):
    base = shared_normal(key)
    return jnp.clip(base, -6.0, 6.0).astype(jnp.bfloat16)


def draw_keys(key, part):
    key = jax.random.fold_in(key, 12)
    own = jax.random.normal(key, (BATCH, HEADS, SEQ_LEN, HEAD_DIM), jnp.float32)
    return jnp.clip(own, -6.0, 6.0).astype(jnp.bfloat16)


def draw_gains(key, part):
    key = jax.random.fold_in(key, 13)
    spread = jax.random.uniform(key, (2, HEAD_DIM), jnp.float32)
    lower = 0.5
    upper = 2.0
    return jnp.exp(jnp.log(lower) + spread * (jnp.log(upper) - jnp.log(lower)))


def shard_levels(rng, shape, pieces, low, largest):
    loudness, own = 1.0, jax.random.fold_in(rng, 6)
    for dim, blocks in pieces:
        draws = jnp.exp(jax.random.uniform(jax.random.fold_in(own, dim), (blocks,), jnp.float32, low / len(pieces), largest / len(pieces)))
        loudness = loudness * jnp.repeat(draws, shape[dim] // blocks).reshape([-1 if axis == dim else 1 for axis in range(len(shape))])
    return loudness


def split_up(number_of, total, most, skew):
    weights = [(1 << 20) // math.isqrt(grade ** skew) + 1 for grade in range(2, number_of + 1)]
    rest, given = total - most - (number_of - 1), [1] * (number_of - 1)
    while rest > 0:
        candidates = [i for i in range(number_of - 1) if given[i] < most]
        pool, remaining = sum([weights[i] for i in candidates]), rest
        for i in candidates:
            addition = min(most - given[i], max(1, remaining * weights[i] // pool), rest)
            given[i] = given[i] + addition
            rest = rest - addition
    return np.array([most] + given)


def ragged_sizes(own_key, amount, total, most, slope):
    if amount == 2:
        one = jax.random.randint(own_key, (), max(1, total - most), min(most, total - 1) + 1)
        return jnp.stack([one, total - one])
    lengths = jnp.asarray(split_up(amount, total, most, slope), jnp.int32)
    twos = (amount - 1) // 2
    source_of, taker = lengths[1:1 + 2 * twos:2], lengths[2:2 + 2 * twos:2]
    margin = jnp.minimum(source_of - 1, most - taker)
    moved = jax.random.randint(jax.random.fold_in(own_key, 1), (twos,), 0, 1 << 20) % (margin + 1)
    lengths = lengths.at[1:1 + 2 * twos:2].set(source_of - moved).at[2:2 + 2 * twos:2].set(taker + moved)
    return lengths[jax.random.permutation(jax.random.fold_in(own_key, 2), amount)]


def normal_values(stream_key, extent, scale, reach, shards=(), kind=jnp.bfloat16):
    values = scale * jax.random.normal(stream_key, extent, jnp.float32)
    if shards:
        values = values * shard_levels(stream_key, extent, shards, -0.22, 0.18)
    return jnp.clip(values, -reach, reach).astype(kind)


def setup_inputs(seed: int = 0) -> dict:
    seeds = jax.random.split(jax.random.key(seed), 8)
    return {
        "queries": draw_queries(jax.random.fold_in(seeds[7], 71), 0),
        "keys": draw_keys(jax.random.fold_in(seeds[7], 71), 0),
        "values": normal_values(seeds[2], (BATCH, HEADS, SEQ_LEN, HEAD_DIM), 1.0, 6.0, ((0, 16), (2, 32))),
        "out_grad": normal_values(seeds[3], (BATCH, HEADS, SEQ_LEN, HEAD_DIM), 1.0, 6.0, ((0, 16), (2, 32))),
        "gains": draw_gains(jax.random.fold_in(seeds[7], 71), 0),
        "keep_order": jax.vmap(lambda own: jax.random.permutation(own, TS))(jax.random.split(seeds[5], BATCH * N_CTX)).reshape((BATCH, N_CTX, TS)).astype(jnp.int32),
        "keep_count": jax.vmap(lambda own: ragged_sizes(own, N_CTX, KEPT, MOST, 2))(jax.random.split(seeds[6], BATCH)).reshape((BATCH, N_CTX)).astype(jnp.int32),
    }


EPS = 1e-06

def normalize(rows, gain):
    upcast = rows.astype(jnp.float32)
    inv_rms = lax.rsqrt(lax.optimization_barrier(jnp.mean(upcast * upcast, axis=-1, keepdims=True)) + EPS)
    unit = upcast * inv_rms
    return ((unit * gain).astype(jnp.bfloat16), unit, inv_rms)

def norm_back(grad_norm, unit, inv_rms, gain):
    tangent = grad_norm * gain
    return (inv_rms * (tangent - unit * lax.optimization_barrier(jnp.mean(tangent * unit, axis=-1, keepdims=True)))).astype(jnp.bfloat16)

def attend_rows(query_rows, key_rows, value_rows, grad_rows, gains):
    scale = query_rows.shape[-1] ** (-0.5)
    query_norm, unit_q, inv_q = normalize(query_rows, gains[0])
    key_norm, unit_k, inv_k = normalize(key_rows, gains[1])
    scores = jnp.dot(query_norm, key_norm.T, preferred_element_type=jnp.float32) * scale
    peak = lax.optimization_barrier(jnp.max(scores, axis=-1, keepdims=True))
    expo = jnp.exp(scores - peak)
    prob = expo / lax.optimization_barrier(jnp.sum(expo, axis=-1, keepdims=True))
    weights = prob.astype(jnp.bfloat16)
    attended = jnp.dot(weights, value_rows, preferred_element_type=jnp.float32).astype(jnp.bfloat16)
    value_grad = jnp.dot(weights.T, grad_rows, preferred_element_type=jnp.float32).astype(jnp.bfloat16)
    dprob = jnp.dot(grad_rows, value_rows.T, preferred_element_type=jnp.float32)
    delta = lax.optimization_barrier(jnp.sum(prob * dprob, axis=-1, keepdims=True))
    dscore = (prob * (dprob - delta)).astype(jnp.bfloat16)
    grad_qn = jnp.dot(dscore, key_norm, preferred_element_type=jnp.float32) * scale
    grad_kn = jnp.dot(dscore.T, query_norm, preferred_element_type=jnp.float32) * scale
    gain_part = jnp.stack([lax.optimization_barrier(jnp.sum(grad_qn * unit_q, axis=0)), lax.optimization_barrier(jnp.sum(grad_kn * unit_k, axis=0))])
    query_grad = norm_back(grad_qn, unit_q, inv_q, gains[0])
    key_grad = norm_back(grad_kn, unit_k, inv_k, gains[1])
    return (attended, query_grad, key_grad, value_grad, gain_part)

def kept_positions(order, counts):
    shard_len = order.shape[1]
    ending = jnp.cumsum(counts).astype(jnp.int32)
    starting = ending - counts
    ranks = jnp.arange(KEPT, dtype=jnp.int32)
    source = lax.optimization_barrier(jnp.sum((ending[None, :] <= ranks[:, None]).astype(jnp.int32), axis=1)).astype(jnp.int32)
    within = (ranks - starting[source]).astype(jnp.int32)
    return (source * shard_len + order[source, within]).astype(jnp.int32)

def reference(queries, keys, values, out_grad, gains, keep_order, keep_count):
    batch, head_count, seq_len, head_dim = queries.shape
    positions = jax.vmap(kept_positions)(keep_order, keep_count)

    def one_pair(pair):
        sample = pair // head_count
        head = pair % head_count
        where = positions[sample]
        result = attend_rows(queries[sample, head][where], keys[sample, head][where], values[sample, head][where], out_grad[sample, head][where], gains)

        def place(rows):
            return jnp.zeros((seq_len, head_dim), jnp.bfloat16).at[where].set(rows)
        return (place(result[0]), place(result[1]), place(result[2]), place(result[3]), result[4])
    outs = lax.map(one_pair, jnp.arange(batch * head_count, dtype=jnp.int32))
    shape = (batch, head_count, seq_len, head_dim)
    gain_grad = lax.optimization_barrier(jnp.sum(outs[4], axis=0))
    return (outs[0].reshape(shape), outs[1].reshape(shape), outs[2].reshape(shape), outs[3].reshape(shape), gain_grad)
```

```python
import jax
import jax.numpy as jnp
from jax import lax
from jax.experimental import pallas as pl
from jax.experimental.pallas import tpu as pltpu
from jax.sharding import PartitionSpec as P

EPS = 1e-06
MESH = pl.DeviceIdType.MESH
BF = jnp.bfloat16
F32 = jnp.float32

DEV = 32
DP = 16
HEADS = 16
TS = 72
HD = 128
KEPT = 1152
MSG = 112
MAIN = 48
HALF = 64
WIDE = DEV * HALF
PAD = KEPT + 64
BLK = 128
BIG = 384


def dot(left, right):
    return jnp.dot(left, right, preferred_element_type=F32)


def dot_last(left, right):
    return lax.dot_general(left, right, (((1,), (1,)), ((), ())), preferred_element_type=F32)


def iota(shape, dim):
    return lax.broadcasted_iota(jnp.int32, shape, dim)


def loop(lo, hi, step, unroll=1):
    def run(index, carry):
        step(index)
        return carry

    lax.fori_loop(lo, hi, run, 0, unroll=unroll)


def kernel(
    gains, order, count_v, count_s, q_hbm, k_hbm, v_hbm, g_hbm,
    o_hbm, dq_hbm, dk_hbm, dv_hbm, gain_out,
    xs, outs, send_qk, send_vg, recv_qk, recv_vg, send_ov, send_dd, recv_ov, recv_dd,
    pack_a, pack_b, unpack, hot_a, hot_b, place_a, place_b,
    prob, prob_b, ds_b, qn, kn, vv, gg, uq, uk, iq, ik, qn_t, gg_t,
    y_o, y_dv, y_dq, y_dk, gsend, gbuf, hsend, hbuf, starts,
    in_sem, out_sem, fs, fr, bs, br, dds, ddr, gs, gr,
):
    me = lax.axis_index("ctx")
    dp = lax.axis_index("dp")
    own_sample = me // HEADS
    scale = HD ** (-0.5)

    def ahead(k):
        return lax.rem(me + k, DEV)

    def behind(k):
        return lax.rem(me + DEV - k, DEV)

    barrier = pltpu.get_barrier_semaphore()
    loop(1, DEV, lambda k: pl.semaphore_signal(
        barrier, inc=1, device_id={"ctx": ahead(k)}, device_id_type=MESH))
    loop(1, DP, lambda k: pl.semaphore_signal(
        barrier, inc=1, device_id={"dp": lax.rem(dp + k, DP)}, device_id_type=MESH))

    loads = [
        pltpu.make_async_copy(ref, xs.at[i], in_sem.at[i])
        for i, ref in enumerate((q_hbm, k_hbm, v_hbm, g_hbm))
    ]
    for load in loads:
        load.start()

    row, slot = iota((MSG, TS), 0), iota((MSG, TS), 1)
    pick_a = ((row == slot) & (row < 54)).astype(F32).astype(BF)
    pick_b = (
        ((row >= HALF) & (slot == row - HALF)) | ((row >= 56) & (row < 62) & (slot == row - 8))
    ).astype(F32).astype(BF)
    for s in range(2):
        tokens = order[s, pl.ds(me, 1), :]
        own_count = count_s[s, me]
        chosen = ((iota((TS, TS), 0) == tokens) & (iota((TS, TS), 1) < own_count))
        chosen = chosen.astype(F32).astype(BF)
        pack_a[s] = dot_last(pick_a, chosen).astype(BF)
        pack_b[s] = dot_last(pick_b, chosen).astype(BF)
        unpack[s, 0:TS] = dot_last(chosen, pick_a).astype(BF)
        unpack[s, TS : 2 * TS] = dot_last(chosen, pick_b).astype(BF)

    for load in loads:
        load.wait()

    def packed(k):
        pair = ahead(k)
        s = pair // HEADS
        first = jnp.concatenate([xs[0, pair], xs[2, pair]], axis=1)
        second = jnp.concatenate([xs[1, pair], xs[3, pair]], axis=1)
        rows = (dot(pack_a[s], first) + dot(pack_b[s], second)).astype(BF)
        return rows[:, :HD], rows[:, HD:]

    recv_qk[0], recv_vg[0] = packed(0)

    def pack(k):
        send_qk[k], send_vg[k] = packed(k)

    loop(1, DEV, pack)
    pl.semaphore_wait(barrier, DEV - 1 + DP - 1)

    def remote(src, dst, send_sem, recv_sem, peer):
        return pltpu.make_async_remote_copy(
            src_ref=src, dst_ref=dst, send_sem=send_sem, recv_sem=recv_sem,
            device_id={"ctx": peer}, device_id_type=MESH)

    def part(src, dst, which, lo, size, sems, semr, peer):
        rows = pl.ds(lo, size)
        return remote(
            src.at[which, rows], dst.at[which, rows], sems, semr, peer
        )

    every = pl.ds(1, DEV - 1)

    def fwd_qk(k):
        return part(send_qk, recv_qk, k, 0, MSG, fs.at[0], fr.at[0], ahead(1))

    loop(1, DEV, lambda k: part(
        send_qk, recv_qk, k, 0, MSG, fs.at[0], fr.at[0], ahead(k)).start())
    loop(1, DEV, lambda k: part(
        send_vg, recv_vg, k, 0, HALF, fs.at[1], fr.at[1], ahead(k)).start())
    loop(1, DEV, lambda k: part(
        send_vg, recv_vg, k, HALF, MAIN, fs.at[2], fr.at[2], ahead(k)).start())
    all_qk = part(send_qk, recv_qk, every, 0, MSG, fs.at[0], fr.at[0], ahead(1))
    all_v = part(send_vg, recv_vg, every, 0, HALF, fs.at[1], fr.at[1], ahead(1))
    all_g = part(send_vg, recv_vg, every, HALF, MAIN, fs.at[2], fr.at[2], ahead(1))

    def add_start(c, total):
        starts[c] = total
        return total + count_s[own_sample, c]

    lax.fori_loop(0, DEV, add_start, jnp.int32(0))
    counts = count_v[pl.ds(own_sample, 1), :].astype(F32)
    upto = (iota((DEV, DEV), 0) <= iota((DEV, DEV), 1)).astype(F32).astype(BF)
    ends = dot(jnp.broadcast_to(counts, (8, DEV)).astype(BF), upto)[0:1, :]
    ranks = iota((KEPT, DEV), 0).astype(F32)
    past = ends <= ranks
    shard = jnp.sum(jnp.where(past, 1.0, 0.0), axis=1, keepdims=True)
    start = jnp.sum(jnp.where(past, counts, 0.0), axis=1, keepdims=True)
    within = iota((KEPT, 1), 0).astype(F32) - start
    place = me.astype(F32) - shard
    place = jnp.where(place < 0.0, place + DEV, place) * HALF
    at_a = (place + within).astype(jnp.int32)
    at_b = (place + jnp.where(within < MAIN, within + 16.0, within - 40.0)).astype(jnp.int32)
    place_a[...] = jnp.broadcast_to(at_a, (KEPT, HD))
    place_b[...] = jnp.broadcast_to(at_b, (KEPT, HD))

    def fill(b):
        rows = pl.ds(pl.multiple_of(b * BLK, BLK), BLK)
        lane = iota((BLK, HD), 1)
        for where, hot in ((place_a, hot_a), (place_b, hot_b)):
            at = where[rows] - lane
            for n in range(WIDE // HD):
                hot[rows, n * HD : (n + 1) * HD] = (at == n * HD).astype(F32).astype(BF)

    loop(0, KEPT // BLK, fill)
    for y in (y_o, y_dv, y_dq, y_dk):
        y[KEPT:PAD] = jnp.zeros((PAD - KEPT, HD), F32)

    def big(b):
        return pl.ds(pl.multiple_of(b * BIG, BIG), BIG)

    def gather(hot, rows, recv, lo):
        return dot(hot[rows], recv[:, lo : lo + HALF].reshape(WIDE, HD))

    all_qk.wait_recv()

    def norms(b):
        rows = big(b)
        for hot, lo, unit_ref, inv_ref, norm_ref, i in (
            (hot_a, 0, uq, iq, qn, 0),
            (hot_b, MAIN, uk, ik, kn, 1),
        ):
            x = gather(hot, rows, recv_qk, lo)
            inv = lax.rsqrt(jnp.mean(x * x, axis=-1, keepdims=True) + EPS)
            unit = x * inv
            unit_ref[rows] = unit
            inv_ref[rows] = jnp.broadcast_to(inv, (BIG, HD))
            norm_ref[rows] = (unit * gains[i : i + 1, :]).astype(BF)

    loop(0, KEPT // BIG, norms)
    qn_t[...] = jnp.transpose(qn[...].astype(F32)).astype(BF)

    def softmax(b):
        rows = pl.ds(pl.multiple_of(b * BLK, BLK), BLK)
        scores = dot_last(qn[rows], kn[...]) * scale
        peak = jnp.max(scores, axis=-1, keepdims=True)
        expo = jnp.exp(scores - peak)
        p = expo / jnp.sum(expo, axis=-1, keepdims=True)
        prob[rows] = p
        prob_b[rows] = p.astype(BF)

    loop(0, KEPT // BLK, softmax)

    all_v.wait_recv()

    def attend(b):
        vv[big(b)] = gather(hot_a, big(b), recv_vg, 0).astype(BF)

    loop(0, KEPT // BIG, attend)

    def attend2(b):
        y_o[big(b)] = dot(prob_b[big(b)], vv[...])

    loop(0, KEPT // BIG, attend2)

    def main_rows(y, k):
        return y[pl.ds(starts[behind(k)], MAIN), :].astype(BF)

    def tail_rows(y, z, k):
        at = pl.ds(starts[behind(k)] + MAIN, 8)
        return jnp.concatenate([y[at, :], z[at, :]], axis=0).astype(BF)

    recv_ov[0, 0:MAIN] = main_rows(y_o, 0)

    def out_main(k):
        send_ov[k, 0:MAIN] = main_rows(y_o, k)

    loop(1, DEV, out_main)
    all_g.wait_send()
    loop(1, DEV, lambda k: part(
        send_ov, recv_ov, k, 0, MAIN, bs.at[0], br.at[0], behind(k)).start())
    all_o = part(send_ov, recv_ov, every, 0, MAIN, bs.at[0], br.at[0], behind(1))

    all_g.wait_recv()

    def cotangents(b):
        gg[big(b)] = gather(hot_b, big(b), recv_vg, MAIN).astype(BF)

    loop(0, KEPT // BIG, cotangents)
    gg_t[...] = jnp.transpose(gg[...].astype(F32)).astype(BF)

    def column(b):
        return pl.ds(pl.multiple_of(b * BIG, BIG), BIG)

    def value_back(b):
        y_dv[big(b)] = jnp.transpose(dot(gg_t[...], prob_b[:, column(b)]))

    loop(0, KEPT // BIG, value_back)
    recv_ov[0, MAIN:HALF] = tail_rows(y_o, y_dv, 0)
    recv_ov[0, HALF:MSG] = main_rows(y_dv, 0)

    def value_main(k):
        send_ov[k, MAIN:HALF] = tail_rows(y_o, y_dv, k)
        send_ov[k, HALF:MSG] = main_rows(y_dv, k)
        part(send_ov, recv_ov, k, MAIN, HALF, bs.at[1], br.at[1], behind(k)).start()

    loop(1, DEV, value_main)
    all_dv = part(send_ov, recv_ov, every, MAIN, HALF, bs.at[1], br.at[1], behind(1))

    def score_back(b):
        rows = pl.ds(pl.multiple_of(b * BLK, BLK), BLK)
        dprob = dot_last(gg[rows], vv[...])
        p = prob[rows]
        delta = jnp.sum(p * dprob, axis=-1, keepdims=True)
        ds_b[rows] = (p * (dprob - delta)).astype(BF)

    loop(0, KEPT // BLK, score_back)

    def norm_back(grad, rows, unit_ref, inv_ref, i, y):
        unit = unit_ref[rows]
        tangent = grad * gains[i : i + 1, :]
        y[rows] = inv_ref[rows] * (
            tangent - unit * jnp.mean(tangent * unit, axis=-1, keepdims=True)
        )
        gsend[i : i + 1, :] += jnp.sum(grad * unit, axis=0, keepdims=True)

    gsend[...] = jnp.zeros_like(gsend)

    def query_back(b):
        grad = dot(ds_b[big(b)], kn[...]) * scale
        norm_back(grad, big(b), uq, iq, 0, y_dq)

    loop(0, KEPT // BIG, query_back)

    def key_back(b):
        grad = jnp.transpose(dot(qn_t[...], ds_b[:, column(b)])) * scale
        norm_back(grad, big(b), uk, ik, 1, y_dk)

    loop(0, KEPT // BIG, key_back)

    def gain_ctx(k):
        return remote(gsend, gbuf.at[k], gs.at[0], gr.at[0], ahead(k))

    gbuf[0] = gsend[...]
    loop(1, DEV, lambda k: gain_ctx(k).start())

    def grad_rows(k):
        return main_rows(y_dq, k), tail_rows(y_dq, y_dk, k), main_rows(y_dk, k)

    recv_dd[0, 0:MAIN], recv_dd[0, MAIN:HALF], recv_dd[0, HALF:MSG] = grad_rows(0)

    def back_dd(k):
        return part(send_dd, recv_dd, k, 0, MSG, dds, ddr.at[k], behind(k))

    def grad_main(k):
        send_dd[k, 0:MAIN], send_dd[k, MAIN:HALF], send_dd[k, HALF:MSG] = grad_rows(k)
        back_dd(k).start()

    loop(1, DEV, grad_main)
    all_dd = part(send_dd, recv_dd, every, 0, MSG, dds, ddr.at[0], behind(1))

    gain_all = pltpu.make_async_remote_copy(
        src_ref=gbuf.at[every], dst_ref=gbuf.at[every], send_sem=gs.at[0], recv_sem=gr.at[0],
        device_id={"ctx": ahead(1)}, device_id_type=MESH)
    gain_all.wait_recv()
    hsend[...] = lax.fori_loop(
        0, DEV, lambda c, acc: acc + gbuf[behind(c)], jnp.zeros((8, HD), F32)
    )
    hbuf[0] = hsend[...]

    def gain_dp(k):
        return pltpu.make_async_remote_copy(
            src_ref=hsend, dst_ref=hbuf.at[k], send_sem=gs.at[1], recv_sem=gr.at[1],
            device_id={"dp": lax.rem(dp + k, DP)}, device_id_type=MESH)

    loop(1, DP, lambda k: gain_dp(k).start())
    others = pl.ds(1, DP - 1)
    gain_dps = pltpu.make_async_remote_copy(
        src_ref=hbuf.at[others], dst_ref=hbuf.at[others], send_sem=gs.at[1], recv_sem=gr.at[1],
        device_id={"dp": lax.rem(dp + 1, DP)}, device_id_type=MESH)

    all_o.wait_recv()
    all_dv.wait_recv()

    def home(k, recv, first, second):
        pair = ahead(k)
        rows = dot(unpack[pair // HEADS], recv[k]).astype(BF)
        outs[first, pair] = rows[:TS]
        outs[second, pair] = rows[TS:]

    loop(0, DEV, lambda k: home(k, recv_ov, 0, 3))
    stores = [
        pltpu.make_async_copy(outs.at[i], ref, out_sem.at[i])
        for i, ref in enumerate((o_hbm, dq_hbm, dk_hbm, dv_hbm))
    ]
    stores[0].start()
    stores[3].start()
    gain_dps.wait_recv()
    total = lax.fori_loop(
        0, DP, lambda c, acc: acc + hbuf[lax.rem(dp + DP - c, DP)], jnp.zeros((8, HD), F32)
    )
    gain_out[...] = total[0:2]
    home(0, recv_dd, 1, 2)

    def last(k):
        back_dd(k).wait_recv()
        home(k, recv_dd, 1, 2)

    loop(1, DEV, last)
    stores[1].start()
    stores[2].start()
    all_qk.wait_send()
    all_v.wait_send()
    all_o.wait_send()
    all_dv.wait_send()
    all_dd.wait_send()
    gain_all.wait_send()
    gain_dps.wait_send()
    for store in stores:
        store.wait()


def body(queries, keys, values, out_grad, gains, keep_order, keep_count):
    pairs = [x.reshape(DEV, TS, HD) for x in (queries, keys, values, out_grad)]
    vmem = pl.BlockSpec(memory_space=pltpu.VMEM)
    smem = pl.BlockSpec(memory_space=pltpu.SMEM)
    hbm = pl.BlockSpec(memory_space=pl.ANY)
    message = pltpu.VMEM((DEV, MSG, HD), BF)
    rows_b, rows_f = pltpu.VMEM((KEPT, HD), BF), pltpu.VMEM((KEPT, HD), F32)
    result = pltpu.VMEM((PAD, HD), F32)
    place = pltpu.VMEM((KEPT, HD), jnp.int32)
    hot = pltpu.VMEM((KEPT, WIDE), BF)
    square_f, square_b = pltpu.VMEM((KEPT, KEPT), F32), pltpu.VMEM((KEPT, KEPT), BF)
    turned = pltpu.VMEM((HD, KEPT), BF)
    dma = pltpu.SemaphoreType.DMA
    out = jax.ShapeDtypeStruct((DEV, TS, HD), BF)
    results = pl.pallas_call(
        kernel,
        out_shape=[out] * 4 + [jax.ShapeDtypeStruct((2, HD), F32)],
        in_specs=[vmem, vmem, vmem, smem] + [hbm] * 4,
        out_specs=[hbm] * 4 + [vmem],
        scratch_shapes=[pltpu.VMEM((4, DEV, TS, HD), BF)] * 2
        + [message] * 8
        + [pltpu.VMEM((2, MSG, TS), BF)] * 2
        + [pltpu.VMEM((2, 2 * TS, MSG), BF)]
        + [hot] * 2
        + [place] * 2
        + [square_f, square_b, square_b]
        + [rows_b] * 4
        + [rows_f] * 4
        + [turned] * 2
        + [result] * 4
        + [pltpu.VMEM((8, HD), F32), pltpu.VMEM((DEV, 8, HD), F32)]
        + [pltpu.VMEM((8, HD), F32), pltpu.VMEM((DP, 8, HD), F32)]
        + [pltpu.SMEM((DEV,), jnp.int32)]
        + [dma((4,)), dma((4,)), dma((3,)), dma((3,)), dma((2,)), dma((2,))]
        + [dma, dma((DEV,)), dma((2,)), dma((2,))],
        compiler_params=pltpu.CompilerParams(
            collective_id=0, has_side_effects=True, vmem_limit_bytes=60 * 1024 * 1024
        ),
    )(gains, keep_order, keep_count, keep_count, *pairs)
    shape = queries.shape
    return tuple(r.reshape(shape) for r in results[:4]) + (results[4],)


def solution(mesh):
    rows = P("dp", None, "ctx", None)
    return jax.shard_map(
        body,
        mesh=mesh,
        in_specs=(rows, rows, rows, rows, P(), P("dp", None, None), P("dp", None)),
        out_specs=(rows, rows, rows, rows, P()),
        check_vma=False,
    )
```

```python
import jax
import jax.numpy as jnp
from jax import lax
from jax.experimental import pallas as pl
from jax.experimental.pallas import tpu as pltpu
from jax.sharding import PartitionSpec as P

EPS = 1e-06
MESH = pl.DeviceIdType.MESH
BF = jnp.bfloat16
F32 = jnp.float32

DEV = 32
DP = 16
HEADS = 16
TS = 72
HD = 128
KEPT = 1152
MSG = 112
MAIN = 48
HALF = 64
WIDE = DEV * HALF
PAD = KEPT + 64
BLK = 128
BIG = 384


def dot(left, right):
    return jnp.dot(left, right, preferred_element_type=F32)


def dot_last(left, right):
    return lax.dot_general(left, right, (((1,), (1,)), ((), ())), preferred_element_type=F32)


def iota(shape, dim):
    return lax.broadcasted_iota(jnp.int32, shape, dim)


def loop(lo, hi, step, unroll=1):
    def run(index, carry):
        step(index)
        return carry

    lax.fori_loop(lo, hi, run, 0, unroll=unroll)


def kernel(
    gains, order, count_v, count_s, q_hbm, k_hbm, v_hbm, g_hbm,
    outs, gain_out,
    xs, send_qk, send_vg, recv_qk, recv_vg, send_ov, send_dd, recv_ov, recv_dd,
    pack_a, pack_b, unpack, hot_a, hot_b, place_a, place_b,
    prob, prob_b, ds_b, qn, kn, vv, gg, uq, uk, iq, ik, qn_t, gg_t,
    y_o, y_dv, y_dq, y_dk, gsend, gbuf, hsend, hbuf, total, starts,
    in_sem, fs, fr, bs, br, dds, ddr, gs, gr,
):
    me = lax.axis_index("ctx")
    dp = lax.axis_index("dp")
    own_sample = me // HEADS
    scale = HD ** (-0.5)

    def ahead(k):
        return lax.rem(me + k, DEV)

    def behind(k):
        return lax.rem(me + DEV - k, DEV)

    def spread(step):
        def both(k):
            step(k)
            step(DEV - k)

        loop(1, DEV // 2, both)
        step(DEV // 2)

    is_hub = me == 0
    barrier = pltpu.get_barrier_semaphore()
    loop(1, DEV, lambda k: pl.semaphore_signal(
        barrier, inc=1, device_id={"ctx": ahead(k)}, device_id_type=MESH))

    @pl.when(is_hub)
    def _():
        loop(1, DP, lambda k: pl.semaphore_signal(
            barrier, inc=1, device_id={"dp": lax.rem(dp + k, DP)}, device_id_type=MESH))

    loads = [
        pltpu.make_async_copy(ref, xs.at[i], in_sem.at[i])
        for i, ref in enumerate((q_hbm, k_hbm, v_hbm, g_hbm))
    ]
    for load in loads:
        load.start()

    row, slot = iota((MSG, TS), 0), iota((MSG, TS), 1)
    pick_a = ((row == slot) & (row < 54)).astype(F32).astype(BF)
    pick_b = (
        ((row >= HALF) & (slot == row - HALF)) | ((row >= 56) & (row < 62) & (slot == row - 8))
    ).astype(F32).astype(BF)
    for s in range(2):
        tokens = order[s, pl.ds(me, 1), :]
        own_count = count_s[s, me]
        chosen = ((iota((TS, TS), 0) == tokens) & (iota((TS, TS), 1) < own_count))
        chosen = chosen.astype(F32).astype(BF)
        pack_a[s] = dot_last(pick_a, chosen).astype(BF)
        pack_b[s] = dot_last(pick_b, chosen).astype(BF)
        unpack[s, 0:TS] = dot_last(chosen, pick_a).astype(BF)
        unpack[s, TS : 2 * TS] = dot_last(chosen, pick_b).astype(BF)

    for load in loads:
        load.wait()

    def packed(k):
        pair = ahead(k)
        s = pair // HEADS
        first = jnp.concatenate([xs[0, pair], xs[2, pair]], axis=1)
        second = jnp.concatenate([xs[1, pair], xs[3, pair]], axis=1)
        rows = (dot(pack_a[s], first) + dot(pack_b[s], second)).astype(BF)
        return rows[:, :HD], rows[:, HD:]

    recv_qk[0], recv_vg[0] = packed(0)

    def pack(k):
        send_qk[k], send_vg[k] = packed(k)

    loop(1, DEV, pack)

    @pl.when(is_hub)
    def _():
        pl.semaphore_wait(barrier, DEV - 1 + DP - 1)

    @pl.when(jnp.logical_not(is_hub))
    def _():
        pl.semaphore_wait(barrier, DEV - 1)

    def remote(src, dst, send_sem, recv_sem, peer):
        return pltpu.make_async_remote_copy(
            src_ref=src, dst_ref=dst, send_sem=send_sem, recv_sem=recv_sem,
            device_id={"ctx": peer}, device_id_type=MESH)

    def part(src, dst, which, lo, size, sems, semr, peer):
        rows = pl.ds(lo, size)
        return remote(
            src.at[which, rows], dst.at[which, rows], sems, semr, peer
        )

    every = pl.ds(1, DEV - 1)

    spread(lambda k: part(
        send_qk, recv_qk, k, 0, MSG, fs.at[0], fr.at[0], ahead(k)).start())
    spread(lambda k: part(
        send_vg, recv_vg, k, 0, HALF, fs.at[1], fr.at[1], ahead(k)).start())
    spread(lambda k: part(
        send_vg, recv_vg, k, HALF, MAIN, fs.at[2], fr.at[2], ahead(k)).start())
    all_qk = part(send_qk, recv_qk, every, 0, MSG, fs.at[0], fr.at[0], ahead(1))
    all_v = part(send_vg, recv_vg, every, 0, HALF, fs.at[1], fr.at[1], ahead(1))
    all_g = part(send_vg, recv_vg, every, HALF, MAIN, fs.at[2], fr.at[2], ahead(1))

    def add_start(c, total):
        starts[c] = total
        return total + count_s[own_sample, c]

    lax.fori_loop(0, DEV, add_start, jnp.int32(0))
    counts = count_v[pl.ds(own_sample, 1), :].astype(F32)
    upto = (iota((DEV, DEV), 0) <= iota((DEV, DEV), 1)).astype(F32).astype(BF)
    ends = dot(jnp.broadcast_to(counts, (8, DEV)).astype(BF), upto)[0:1, :]
    ranks = iota((KEPT, DEV), 0).astype(F32)
    past = ends <= ranks
    shard = jnp.sum(jnp.where(past, 1.0, 0.0), axis=1, keepdims=True)
    start = jnp.sum(jnp.where(past, counts, 0.0), axis=1, keepdims=True)
    within = iota((KEPT, 1), 0).astype(F32) - start
    place = me.astype(F32) - shard
    place = jnp.where(place < 0.0, place + DEV, place) * HALF
    at_a = (place + within).astype(jnp.int32)
    at_b = (place + jnp.where(within < MAIN, within + 16.0, within - 40.0)).astype(jnp.int32)
    place_a[...] = jnp.broadcast_to(at_a, (KEPT, HD))
    place_b[...] = jnp.broadcast_to(at_b, (KEPT, HD))

    def fill(b):
        rows = pl.ds(pl.multiple_of(b * BLK, BLK), BLK)
        lane = iota((BLK, HD), 1)
        for where, hot in ((place_a, hot_a), (place_b, hot_b)):
            at = where[rows] - lane
            for n in range(WIDE // HD):
                hot[rows, n * HD : (n + 1) * HD] = (at == n * HD).astype(F32).astype(BF)

    loop(0, KEPT // BLK, fill)
    for y in (y_o, y_dv, y_dq, y_dk):
        y[KEPT:PAD] = jnp.zeros((PAD - KEPT, HD), F32)

    def big(b):
        return pl.ds(pl.multiple_of(b * BIG, BIG), BIG)

    def gather(hot, rows, recv, lo):
        return dot(hot[rows], recv[:, lo : lo + HALF].reshape(WIDE, HD))

    all_qk.wait_recv()

    def norms(b):
        rows = big(b)
        for hot, lo, unit_ref, inv_ref, norm_ref, i in (
            (hot_a, 0, uq, iq, qn, 0),
            (hot_b, MAIN, uk, ik, kn, 1),
        ):
            x = gather(hot, rows, recv_qk, lo)
            inv = lax.rsqrt(jnp.mean(x * x, axis=-1, keepdims=True) + EPS)
            unit = x * inv
            unit_ref[rows] = unit
            inv_ref[rows] = jnp.broadcast_to(inv, (BIG, HD))
            norm_ref[rows] = (unit * gains[i : i + 1, :]).astype(BF)

    loop(0, KEPT // BIG, norms)
    qn_t[...] = jnp.transpose(qn[...].astype(F32)).astype(BF)

    def softmax(b):
        rows = pl.ds(pl.multiple_of(b * BLK, BLK), BLK)
        scores = dot_last(qn[rows], kn[...]) * scale
        peak = jnp.max(scores, axis=-1, keepdims=True)
        expo = jnp.exp(scores - peak)
        p = expo / jnp.sum(expo, axis=-1, keepdims=True)
        prob[rows] = p
        prob_b[rows] = p.astype(BF)

    loop(0, KEPT // BLK, softmax)

    all_v.wait_recv()

    def attend(b):
        vv[big(b)] = gather(hot_a, big(b), recv_vg, 0).astype(BF)

    loop(0, KEPT // BIG, attend)

    def attend2(b):
        y_o[big(b)] = dot(prob_b[big(b)], vv[...])

    loop(0, KEPT // BIG, attend2)

    def main_rows(y, k):
        return y[pl.ds(starts[behind(k)], MAIN), :].astype(BF)

    def tail_rows(y, z, k):
        at = pl.ds(starts[behind(k)] + MAIN, 8)
        return jnp.concatenate([y[at, :], z[at, :]], axis=0).astype(BF)

    recv_ov[0, 0:MAIN] = main_rows(y_o, 0)

    def out_main(k):
        send_ov[k, 0:MAIN] = main_rows(y_o, k)

    loop(1, DEV, out_main)
    all_g.wait_send()
    spread(lambda k: part(
        send_ov, recv_ov, k, 0, MAIN, bs.at[0], br.at[0], behind(k)).start())
    all_o = part(send_ov, recv_ov, every, 0, MAIN, bs.at[0], br.at[0], behind(1))

    all_g.wait_recv()

    def cotangents(b):
        gg[big(b)] = gather(hot_b, big(b), recv_vg, MAIN).astype(BF)

    loop(0, KEPT // BIG, cotangents)
    gg_t[...] = jnp.transpose(gg[...].astype(F32)).astype(BF)

    def column(b):
        return pl.ds(pl.multiple_of(b * BIG, BIG), BIG)

    def value_back(b):
        y_dv[big(b)] = jnp.transpose(dot(gg_t[...], prob_b[:, column(b)]))

    loop(0, KEPT // BIG, value_back)
    recv_ov[0, MAIN:HALF] = tail_rows(y_o, y_dv, 0)
    recv_ov[0, HALF:MSG] = main_rows(y_dv, 0)

    def value_main(k):
        send_ov[k, MAIN:HALF] = tail_rows(y_o, y_dv, k)
        send_ov[k, HALF:MSG] = main_rows(y_dv, k)
        part(send_ov, recv_ov, k, MAIN, HALF, bs.at[1], br.at[1], behind(k)).start()

    spread(value_main)
    all_dv = part(send_ov, recv_ov, every, MAIN, HALF, bs.at[1], br.at[1], behind(1))

    def score_back(b):
        rows = pl.ds(pl.multiple_of(b * BLK, BLK), BLK)
        dprob = dot_last(gg[rows], vv[...])
        p = prob[rows]
        delta = jnp.sum(p * dprob, axis=-1, keepdims=True)
        ds_b[rows] = (p * (dprob - delta)).astype(BF)

    loop(0, KEPT // BLK, score_back)

    def norm_back(grad, rows, unit_ref, inv_ref, i, y):
        unit = unit_ref[rows]
        tangent = grad * gains[i : i + 1, :]
        y[rows] = inv_ref[rows] * (
            tangent - unit * jnp.mean(tangent * unit, axis=-1, keepdims=True)
        )
        gsend[i : i + 1, :] += jnp.sum(grad * unit, axis=0, keepdims=True)

    gsend[...] = jnp.zeros_like(gsend)

    def query_back(b):
        grad = dot(ds_b[big(b)], kn[...]) * scale
        norm_back(grad, big(b), uq, iq, 0, y_dq)

    loop(0, KEPT // BIG, query_back)

    def key_back(b):
        grad = jnp.transpose(dot(qn_t[...], ds_b[:, column(b)])) * scale
        norm_back(grad, big(b), uk, ik, 1, y_dk)

    loop(0, KEPT // BIG, key_back)

    to_hub = remote(gsend, gbuf.at[me], gs.at[0], gr.at[0], 0)
    from_devs = remote(gbuf.at[every], gbuf.at[every], gs.at[0], gr.at[0], 0)
    others = pl.ds(1, DP - 1)

    def to_group(k):
        return remote(total.at[0], total.at[1], gs.at[2], gr.at[2], ahead(k))

    def between(src, dst, k):
        return pltpu.make_async_remote_copy(
            src_ref=src, dst_ref=dst, send_sem=gs.at[1], recv_sem=gr.at[1],
            device_id={"dp": lax.rem(dp + k, DP)}, device_id_type=MESH)

    @pl.when(jnp.logical_not(is_hub))
    def _():
        to_hub.start()

    @pl.when(is_hub)
    def _():
        gbuf[0] = gsend[...]
        from_devs.wait_recv()
        hsend[...] = lax.fori_loop(
            0, DEV, lambda c, acc: acc + gbuf[c], jnp.zeros((8, HD), F32)
        )
        hbuf[0] = hsend[...]
        loop(1, DP, lambda k: between(hsend, hbuf.at[k], k).start())
        between(hbuf.at[others], hbuf.at[others], 1).wait_recv()
        total[0] = lax.fori_loop(
            0, DP, lambda c, acc: acc + hbuf[lax.rem(dp + DP - c, DP)], jnp.zeros((8, HD), F32)
        )
        total[1] = total[0]
        loop(1, DEV, lambda k: to_group(k).start())

    def grad_rows(k):
        return main_rows(y_dq, k), tail_rows(y_dq, y_dk, k), main_rows(y_dk, k)

    recv_dd[0, 0:MAIN], recv_dd[0, MAIN:HALF], recv_dd[0, HALF:MSG] = grad_rows(0)

    def back_dd(k):
        return part(send_dd, recv_dd, k, 0, MSG, dds, ddr.at[k], behind(k))

    def grad_main(k):
        send_dd[k, 0:MAIN], send_dd[k, MAIN:HALF], send_dd[k, HALF:MSG] = grad_rows(k)
        back_dd(k).start()

    spread(grad_main)
    all_dd = part(send_dd, recv_dd, every, 0, MSG, dds, ddr.at[0], behind(1))

    all_o.wait_recv()
    all_dv.wait_recv()

    def home(k, recv, first, second):
        pair = ahead(k)
        rows = dot(unpack[pair // HEADS], recv[k]).astype(BF)
        outs[first, pair] = rows[:TS]
        outs[second, pair] = rows[TS:]

    loop(0, DEV, lambda k: home(k, recv_ov, 0, 3))
    home(0, recv_dd, 1, 2)

    def last(k):
        back_dd(k).wait_recv()
        home(k, recv_dd, 1, 2)

    spread(last)

    @pl.when(is_hub)
    def _():
        between(hbuf.at[others], hbuf.at[others], 1).wait_send()
        loop(1, DEV, lambda k: to_group(k).wait_send())

    @pl.when(jnp.logical_not(is_hub))
    def _():
        to_hub.wait_send()
        to_group(1).wait_recv()

    gain_out[...] = total[1, 0:2]
    all_qk.wait_send()
    all_v.wait_send()
    all_o.wait_send()
    all_dv.wait_send()
    all_dd.wait_send()


def deal(merged, gain, o_out, dq_out, dk_out, dv_out, gain_out, sem):
    copies = [
        pltpu.make_async_copy(merged.at[i], ref, sem.at[i])
        for i, ref in enumerate((o_out, dq_out, dk_out, dv_out))
    ]
    for copy in copies:
        copy.start()
    gain_out[...] = gain[...]
    for copy in copies:
        copy.wait()


def body(queries, keys, values, out_grad, gains, keep_order, keep_count):
    pairs = [x.reshape(DEV, TS, HD) for x in (queries, keys, values, out_grad)]
    vmem = pl.BlockSpec(memory_space=pltpu.VMEM)
    smem = pl.BlockSpec(memory_space=pltpu.SMEM)
    hbm = pl.BlockSpec(memory_space=pl.ANY)
    message = pltpu.VMEM((DEV, MSG, HD), BF)
    rows_b, rows_f = pltpu.VMEM((KEPT, HD), BF), pltpu.VMEM((KEPT, HD), F32)
    result = pltpu.VMEM((PAD, HD), F32)
    place = pltpu.VMEM((KEPT, HD), jnp.int32)
    hot = pltpu.VMEM((KEPT, WIDE), BF)
    square_f, square_b = pltpu.VMEM((KEPT, KEPT), F32), pltpu.VMEM((KEPT, KEPT), BF)
    turned = pltpu.VMEM((HD, KEPT), BF)
    dma = pltpu.SemaphoreType.DMA
    out = jax.ShapeDtypeStruct((DEV, TS, HD), BF)
    gain_shape = jax.ShapeDtypeStruct((2, HD), F32)
    merged, gain = pl.pallas_call(
        kernel,
        out_shape=[pltpu.VMEM((4, DEV, TS, HD), BF), pltpu.VMEM((2, HD), F32)],
        in_specs=[vmem, vmem, vmem, smem] + [hbm] * 4,
        out_specs=[vmem, vmem],
        scratch_shapes=[pltpu.VMEM((4, DEV, TS, HD), BF)]
        + [message] * 8
        + [pltpu.VMEM((2, MSG, TS), BF)] * 2
        + [pltpu.VMEM((2, 2 * TS, MSG), BF)]
        + [hot] * 2
        + [place] * 2
        + [square_f, square_b, square_b]
        + [rows_b] * 4
        + [rows_f] * 4
        + [turned] * 2
        + [result] * 4
        + [pltpu.VMEM((8, HD), F32), pltpu.VMEM((DEV, 8, HD), F32)]
        + [pltpu.VMEM((8, HD), F32), pltpu.VMEM((DP, 8, HD), F32)]
        + [pltpu.VMEM((2, 8, HD), F32)]
        + [pltpu.SMEM((DEV,), jnp.int32)]
        + [dma((4,)), dma((3,)), dma((3,)), dma((2,)), dma((2,))]
        + [dma, dma((DEV,)), dma((3,)), dma((3,))],
        compiler_params=pltpu.CompilerParams(
            collective_id=0, has_side_effects=True, vmem_limit_bytes=60 * 1024 * 1024
        ),
    )(gains, keep_order, keep_count, keep_count, *pairs)
    results = pl.pallas_call(
        deal,
        out_shape=[out] * 4 + [gain_shape],
        in_specs=[vmem, vmem],
        out_specs=[hbm] * 4 + [vmem],
        scratch_shapes=[dma((4,))],
        compiler_params=pltpu.CompilerParams(vmem_limit_bytes=8 * 1024 * 1024),
    )(merged, gain)
    shape = queries.shape
    return tuple(r.reshape(shape) for r in results[:4]) + (results[4],)


def solution(mesh):
    rows = P("dp", None, "ctx", None)
    return jax.shard_map(
        body,
        mesh=mesh,
        in_specs=(rows, rows, rows, rows, P(), P("dp", None, None), P("dp", None)),
        out_specs=(rows, rows, rows, rows, P()),
        check_vma=False,
    )
```

```python
import jax
import jax.numpy as jnp
from jax import lax
from jax.experimental import pallas as pl
from jax.experimental.pallas import tpu as pltpu
from jax.sharding import PartitionSpec as P

EPS = 1e-06
MESH = pl.DeviceIdType.MESH
BF = jnp.bfloat16
F32 = jnp.float32

DEV = 32
DP = 16
HEADS = 16
TS = 72
HD = 128
KEPT = 1152
MSG = 112
MAIN = 48
HALF = 64
WIDE = DEV * HALF
PAD = KEPT + 64
BLK = 128
BIG = 384


def dot(left, right):
    return jnp.dot(left, right, preferred_element_type=F32)


def dot_last(left, right):
    return lax.dot_general(left, right, (((1,), (1,)), ((), ())), preferred_element_type=F32)


def iota(shape, dim):
    return lax.broadcasted_iota(jnp.int32, shape, dim)


def loop(lo, hi, step, unroll=1):
    def run(index, carry):
        step(index)
        return carry

    lax.fori_loop(lo, hi, run, 0, unroll=unroll)


def kernel(
    gains, order, count_v, count_s, q_hbm, k_hbm, v_hbm, g_hbm,
    outs, gain_out,
    xs, send_qk, send_vg, recv_qk, recv_vg, send_ov, send_dd, recv_ov, recv_dd,
    pack_a, pack_b, unpack, hot_a, hot_b, place_a, place_b,
    prob, prob_b, ds_b, qn, kn, vv, gg, uq, uk, iq, ik, qn_t, gg_t,
    y_o, y_dv, y_dq, y_dk, gsend, gbuf, hsend, hbuf, total, starts,
    met, in_sem, fs, fr, bs, br, dds, ddr, gs, gr,
):
    me = lax.axis_index("ctx")
    dp = lax.axis_index("dp")
    own_sample = me // HEADS
    scale = HD ** (-0.5)

    def ahead(k):
        return lax.rem(me + k, DEV)

    def behind(k):
        return lax.rem(me + DEV - k, DEV)

    def pairs(lo, hi, step):
        def both(k):
            step(k)
            step(DEV - k)

        loop(lo, hi, both)

    def spread(step):
        pairs(1, DEV // 2, step)
        step(DEV // 2)

    is_hub = me == 0
    barrier = pltpu.get_barrier_semaphore()

    def greet(k):
        @pl.when(ahead(k) != 0)
        def _():
            pl.semaphore_signal(
                barrier, inc=1, device_id={"ctx": ahead(k)}, device_id_type=MESH
            )

    loop(1, DEV, greet)

    @pl.when(is_hub)
    def _():
        loop(1, DP, lambda k: pl.semaphore_signal(
            barrier, inc=1, device_id={"dp": lax.rem(dp + k, DP)}, device_id_type=MESH))

    loads = [
        pltpu.make_async_copy(ref, xs.at[i], in_sem.at[i])
        for i, ref in enumerate((q_hbm, k_hbm, v_hbm, g_hbm))
    ]
    for load in loads:
        load.start()

    row, slot = iota((MSG, TS), 0), iota((MSG, TS), 1)
    pick_a = ((row == slot) & (row < 54)).astype(F32).astype(BF)
    pick_b = (
        ((row >= HALF) & (slot == row - HALF)) | ((row >= 56) & (row < 62) & (slot == row - 8))
    ).astype(F32).astype(BF)
    for s in range(2):
        tokens = order[s, pl.ds(me, 1), :]
        own_count = count_s[s, me]
        chosen = ((iota((TS, TS), 0) == tokens) & (iota((TS, TS), 1) < own_count))
        chosen = chosen.astype(F32).astype(BF)
        pack_a[s] = dot_last(pick_a, chosen).astype(BF)
        pack_b[s] = dot_last(pick_b, chosen).astype(BF)
        unpack[s, 0:TS] = dot_last(chosen, pick_a).astype(BF)
        unpack[s, TS : 2 * TS] = dot_last(chosen, pick_b).astype(BF)

    for load in loads:
        load.wait()

    def packed(k):
        pair = ahead(k)
        s = pair // HEADS
        first = jnp.concatenate([xs[0, pair], xs[2, pair]], axis=1)
        second = jnp.concatenate([xs[1, pair], xs[3, pair]], axis=1)
        rows = (dot(pack_a[s], first) + dot(pack_b[s], second)).astype(BF)
        return rows[:, :HD], rows[:, HD:]

    @pl.when(jnp.logical_not(is_hub))
    def _():
        pl.semaphore_wait(barrier, DEV - 1)
        pl.semaphore_signal(met, inc=1, device_id={"ctx": 0}, device_id_type=MESH)

    @pl.when(is_hub)
    def _():
        pl.semaphore_wait(met, DEV - 1)

    def remote(src, dst, send_sem, recv_sem, peer):
        return pltpu.make_async_remote_copy(
            src_ref=src, dst_ref=dst, send_sem=send_sem, recv_sem=recv_sem,
            device_id={"ctx": peer}, device_id_type=MESH)

    def part(src, dst, which, lo, size, sems, semr, peer):
        rows = pl.ds(lo, size)
        return remote(
            src.at[which, rows], dst.at[which, rows], sems, semr, peer
        )

    every = pl.ds(1, DEV - 1)

    def pack(k):
        send_qk[k], send_vg[k] = packed(k)
        part(send_qk, recv_qk, k, 0, MSG, fs.at[0], fr.at[0], ahead(k)).start()

    spread(pack)
    spread(lambda k: part(
        send_vg, recv_vg, k, 0, HALF, fs.at[1], fr.at[1], ahead(k)).start())
    spread(lambda k: part(
        send_vg, recv_vg, k, HALF, MAIN, fs.at[2], fr.at[2], ahead(k)).start())
    all_qk = part(send_qk, recv_qk, every, 0, MSG, fs.at[0], fr.at[0], ahead(1))
    all_v = part(send_vg, recv_vg, every, 0, HALF, fs.at[1], fr.at[1], ahead(1))
    all_g = part(send_vg, recv_vg, every, HALF, MAIN, fs.at[2], fr.at[2], ahead(1))

    recv_qk[0], recv_vg[0] = packed(0)

    def add_start(c, total):
        starts[c] = total
        return total + count_s[own_sample, c]

    lax.fori_loop(0, DEV, add_start, jnp.int32(0))
    counts = count_v[pl.ds(own_sample, 1), :].astype(F32)
    upto = (iota((DEV, DEV), 0) <= iota((DEV, DEV), 1)).astype(F32).astype(BF)
    ends = dot(jnp.broadcast_to(counts, (8, DEV)).astype(BF), upto)[0:1, :]
    ranks = iota((KEPT, DEV), 0).astype(F32)
    past = ends <= ranks
    shard = jnp.sum(jnp.where(past, 1.0, 0.0), axis=1, keepdims=True)
    start = jnp.sum(jnp.where(past, counts, 0.0), axis=1, keepdims=True)
    within = iota((KEPT, 1), 0).astype(F32) - start
    place = me.astype(F32) - shard
    place = jnp.where(place < 0.0, place + DEV, place) * HALF
    at_a = (place + within).astype(jnp.int32)
    at_b = (place + jnp.where(within < MAIN, within + 16.0, within - 40.0)).astype(jnp.int32)
    place_a[...] = jnp.broadcast_to(at_a, (KEPT, HD))
    place_b[...] = jnp.broadcast_to(at_b, (KEPT, HD))

    def fill(b):
        rows = pl.ds(pl.multiple_of(b * BLK, BLK), BLK)
        lane = iota((BLK, HD), 1)
        for where, hot in ((place_a, hot_a), (place_b, hot_b)):
            at = where[rows] - lane
            for n in range(WIDE // HD):
                hot[rows, n * HD : (n + 1) * HD] = (at == n * HD).astype(F32).astype(BF)

    loop(0, KEPT // BLK, fill)
    for y in (y_o, y_dv, y_dq, y_dk):
        y[KEPT:PAD] = jnp.zeros((PAD - KEPT, HD), F32)

    def big(b):
        return pl.ds(pl.multiple_of(b * BIG, BIG), BIG)

    def gather(hot, rows, recv, lo):
        return dot(hot[rows], recv[:, lo : lo + HALF].reshape(WIDE, HD))

    all_qk.wait_recv()

    def norms(b):
        rows = big(b)
        for hot, lo, unit_ref, inv_ref, norm_ref, i in (
            (hot_a, 0, uq, iq, qn, 0),
            (hot_b, MAIN, uk, ik, kn, 1),
        ):
            x = gather(hot, rows, recv_qk, lo)
            inv = lax.rsqrt(jnp.mean(x * x, axis=-1, keepdims=True) + EPS)
            unit = x * inv
            unit_ref[rows] = unit
            inv_ref[rows] = jnp.broadcast_to(inv, (BIG, HD))
            norm_ref[rows] = (unit * gains[i : i + 1, :]).astype(BF)

    loop(0, KEPT // BIG, norms)
    qn_t[...] = jnp.transpose(qn[...].astype(F32)).astype(BF)

    def softmax(b):
        rows = pl.ds(pl.multiple_of(b * BLK, BLK), BLK)
        scores = dot_last(qn[rows], kn[...]) * scale
        peak = jnp.max(scores, axis=-1, keepdims=True)
        expo = jnp.exp(scores - peak)
        p = expo / jnp.sum(expo, axis=-1, keepdims=True)
        prob[rows] = p
        prob_b[rows] = p.astype(BF)

    loop(0, KEPT // BLK, softmax)

    all_v.wait_recv()

    def attend(b):
        vv[big(b)] = gather(hot_a, big(b), recv_vg, 0).astype(BF)

    loop(0, KEPT // BIG, attend)

    def attend2(b):
        y_o[big(b)] = dot(prob_b[big(b)], vv[...])

    loop(0, KEPT // BIG, attend2)

    def main_rows(y, k):
        return y[pl.ds(starts[behind(k)], MAIN), :].astype(BF)

    def tail_rows(y, z, k):
        at = pl.ds(starts[behind(k)] + MAIN, 8)
        return jnp.concatenate([y[at, :], z[at, :]], axis=0).astype(BF)

    recv_ov[0, 0:MAIN] = main_rows(y_o, 0)

    def out_main(k):
        send_ov[k, 0:MAIN] = main_rows(y_o, k)

    loop(1, DEV, out_main)
    all_g.wait_send()
    spread(lambda k: part(
        send_ov, recv_ov, k, 0, MAIN, bs.at[0], br.at[0], behind(k)).start())
    all_o = part(send_ov, recv_ov, every, 0, MAIN, bs.at[0], br.at[0], behind(1))

    all_g.wait_recv()

    def cotangents(b):
        gg[big(b)] = gather(hot_b, big(b), recv_vg, MAIN).astype(BF)

    loop(0, KEPT // BIG, cotangents)
    gg_t[...] = jnp.transpose(gg[...].astype(F32)).astype(BF)

    def column(b):
        return pl.ds(pl.multiple_of(b * BIG, BIG), BIG)

    def value_back(b):
        y_dv[big(b)] = jnp.transpose(dot(gg_t[...], prob_b[:, column(b)]))

    loop(0, KEPT // BIG, value_back)
    recv_ov[0, MAIN:HALF] = tail_rows(y_o, y_dv, 0)
    recv_ov[0, HALF:MSG] = main_rows(y_dv, 0)

    def value_main(k):
        send_ov[k, MAIN:HALF] = tail_rows(y_o, y_dv, k)
        send_ov[k, HALF:MSG] = main_rows(y_dv, k)
        part(send_ov, recv_ov, k, MAIN, HALF, bs.at[1], br.at[1], behind(k)).start()

    spread(value_main)
    all_dv = part(send_ov, recv_ov, every, MAIN, HALF, bs.at[1], br.at[1], behind(1))

    def score_back(b):
        rows = pl.ds(pl.multiple_of(b * BLK, BLK), BLK)
        dprob = dot_last(gg[rows], vv[...])
        p = prob[rows]
        delta = jnp.sum(p * dprob, axis=-1, keepdims=True)
        ds_b[rows] = (p * (dprob - delta)).astype(BF)

    loop(0, KEPT // BLK, score_back)

    def norm_back(grad, rows, unit_ref, inv_ref, i, y):
        unit = unit_ref[rows]
        tangent = grad * gains[i : i + 1, :]
        y[rows] = inv_ref[rows] * (
            tangent - unit * jnp.mean(tangent * unit, axis=-1, keepdims=True)
        )
        gsend[i : i + 1, :] += jnp.sum(grad * unit, axis=0, keepdims=True)

    gsend[...] = jnp.zeros_like(gsend)

    def query_back(b):
        grad = dot(ds_b[big(b)], kn[...]) * scale
        norm_back(grad, big(b), uq, iq, 0, y_dq)

    loop(0, KEPT // BIG, query_back)

    def key_back(b):
        grad = jnp.transpose(dot(qn_t[...], ds_b[:, column(b)])) * scale
        norm_back(grad, big(b), uk, ik, 1, y_dk)

    loop(0, KEPT // BIG, key_back)

    to_hub = remote(gsend, gbuf.at[me], gs.at[0], gr.at[0], 0)
    from_devs = remote(gbuf.at[every], gbuf.at[every], gs.at[0], gr.at[0], 0)
    others = pl.ds(1, DP - 1)

    def to_group(k):
        return remote(total.at[0], total.at[1], gs.at[2], gr.at[2], ahead(k))

    def between(src, dst, k):
        return pltpu.make_async_remote_copy(
            src_ref=src, dst_ref=dst, send_sem=gs.at[1], recv_sem=gr.at[1],
            device_id={"dp": lax.rem(dp + k, DP)}, device_id_type=MESH)

    @pl.when(jnp.logical_not(is_hub))
    def _():
        to_hub.start()

    def grad_rows(k):
        return main_rows(y_dq, k), tail_rows(y_dq, y_dk, k), main_rows(y_dk, k)

    recv_dd[0, 0:MAIN], recv_dd[0, MAIN:HALF], recv_dd[0, HALF:MSG] = grad_rows(0)

    def back_dd(k):
        return part(send_dd, recv_dd, k, 0, MSG, dds, ddr.at[k], behind(k))

    def grad_main(k):
        send_dd[k, 0:MAIN], send_dd[k, MAIN:HALF], send_dd[k, HALF:MSG] = grad_rows(k)
        back_dd(k).start()

    spread(grad_main)

    @pl.when(is_hub)
    def _():
        gbuf[0] = gsend[...]
        from_devs.wait_recv()
        hsend[...] = lax.fori_loop(
            0, DEV, lambda c, acc: acc + gbuf[c], jnp.zeros((8, HD), F32)
        )
        hbuf[0] = hsend[...]
        pl.semaphore_wait(barrier, DP - 1)
        loop(1, DP, lambda k: between(hsend, hbuf.at[k], k).start())

    all_dd = part(send_dd, recv_dd, every, 0, MSG, dds, ddr.at[0], behind(1))

    all_o.wait_recv()
    all_dv.wait_recv()

    def home(k, recv, first, second):
        pair = ahead(k)
        rows = dot(unpack[pair // HEADS], recv[k]).astype(BF)
        outs[first, pair] = rows[:TS]
        outs[second, pair] = rows[TS:]

    loop(0, DEV, lambda k: home(k, recv_ov, 0, 3))
    @pl.when(is_hub)
    def _():
        between(hbuf.at[others], hbuf.at[others], 1).wait_recv()
        total[0] = lax.fori_loop(
            0, DP, lambda c, acc: acc + hbuf[lax.rem(dp + DP - c, DP)], jnp.zeros((8, HD), F32)
        )
        total[1] = total[0]
        loop(1, DEV, lambda k: to_group(k).start())

    home(0, recv_dd, 1, 2)

    def last(k):
        back_dd(k).wait_recv()
        home(k, recv_dd, 1, 2)

    spread(last)

    @pl.when(is_hub)
    def _():
        between(hbuf.at[others], hbuf.at[others], 1).wait_send()
        loop(1, DEV, lambda k: to_group(k).wait_send())

    @pl.when(jnp.logical_not(is_hub))
    def _():
        to_hub.wait_send()
        to_group(1).wait_recv()

    gain_out[...] = total[1, 0:2]
    all_qk.wait_send()
    all_v.wait_send()
    all_o.wait_send()
    all_dv.wait_send()
    all_dd.wait_send()


def deal(merged, gain, o_out, dq_out, dk_out, dv_out, gain_out, sem):
    copies = [
        pltpu.make_async_copy(merged.at[i, rows], ref.at[rows], sem.at[i, n])
        for n in range(4)
        for rows in (pl.ds(n * (DEV // 4), DEV // 4),)
        for i, ref in enumerate((o_out, dq_out, dk_out, dv_out))
    ]
    for copy in copies:
        copy.start()
    gain_out[...] = gain[...]
    for copy in copies:
        copy.wait()


def body(queries, keys, values, out_grad, gains, keep_order, keep_count):
    pairs = [x.reshape(DEV, TS, HD) for x in (queries, keys, values, out_grad)]
    vmem = pl.BlockSpec(memory_space=pltpu.VMEM)
    smem = pl.BlockSpec(memory_space=pltpu.SMEM)
    hbm = pl.BlockSpec(memory_space=pl.ANY)
    message = pltpu.VMEM((DEV, MSG, HD), BF)
    rows_b, rows_f = pltpu.VMEM((KEPT, HD), BF), pltpu.VMEM((KEPT, HD), F32)
    result = pltpu.VMEM((PAD, HD), F32)
    place = pltpu.VMEM((KEPT, HD), jnp.int32)
    hot = pltpu.VMEM((KEPT, WIDE), BF)
    square_f, square_b = pltpu.VMEM((KEPT, KEPT), F32), pltpu.VMEM((KEPT, KEPT), BF)
    turned = pltpu.VMEM((HD, KEPT), BF)
    dma = pltpu.SemaphoreType.DMA
    out = jax.ShapeDtypeStruct((DEV, TS, HD), BF)
    gain_shape = jax.ShapeDtypeStruct((2, HD), F32)
    merged, gain = pl.pallas_call(
        kernel,
        out_shape=[pltpu.VMEM((4, DEV, TS, HD), BF), pltpu.VMEM((2, HD), F32)],
        in_specs=[vmem, vmem, vmem, smem] + [hbm] * 4,
        out_specs=[vmem, vmem],
        scratch_shapes=[pltpu.VMEM((4, DEV, TS, HD), BF)]
        + [message] * 8
        + [pltpu.VMEM((2, MSG, TS), BF)] * 2
        + [pltpu.VMEM((2, 2 * TS, MSG), BF)]
        + [hot] * 2
        + [place] * 2
        + [square_f, square_b, square_b]
        + [rows_b] * 4
        + [rows_f] * 4
        + [turned] * 2
        + [result] * 4
        + [pltpu.VMEM((8, HD), F32), pltpu.VMEM((DEV, 8, HD), F32)]
        + [pltpu.VMEM((8, HD), F32), pltpu.VMEM((DP, 8, HD), F32)]
        + [pltpu.VMEM((2, 8, HD), F32)]
        + [pltpu.SMEM((DEV,), jnp.int32)]
        + [pltpu.SemaphoreType.REGULAR, dma((4,)), dma((3,)), dma((3,)), dma((2,)), dma((2,))]
        + [dma, dma((DEV,)), dma((3,)), dma((3,))],
        compiler_params=pltpu.CompilerParams(
            collective_id=0, has_side_effects=True, vmem_limit_bytes=60 * 1024 * 1024
        ),
    )(gains, keep_order, keep_count, keep_count, *pairs)
    results = pl.pallas_call(
        deal,
        out_shape=[out] * 4 + [gain_shape],
        in_specs=[vmem, vmem],
        out_specs=[hbm] * 4 + [vmem],
        scratch_shapes=[dma((4, 4))],
        compiler_params=pltpu.CompilerParams(vmem_limit_bytes=8 * 1024 * 1024),
    )(merged, gain)
    shape = queries.shape
    return tuple(r.reshape(shape) for r in results[:4]) + (results[4],)


def solution(mesh):
    rows = P("dp", None, "ctx", None)
    return jax.shard_map(
        body,
        mesh=mesh,
        in_specs=(rows, rows, rows, rows, P(), P("dp", None, None), P("dp", None)),
        out_specs=(rows, rows, rows, rows, P()),
        check_vma=False,
    )
```

```python
import jax
import jax.numpy as jnp
from jax import lax
from jax.experimental import pallas as pl
from jax.experimental.pallas import tpu as pltpu
from jax.sharding import PartitionSpec as P

EPS = 1e-06
MESH = pl.DeviceIdType.MESH
BF = jnp.bfloat16
F32 = jnp.float32

DEV = 32
NY, NX = 8, 4
DP = 16
HEADS = 16
TS = 72
HD = 128
KEPT = 1152
MSG = 112
MAIN = 48
HALF = 64
WIDE = DEV * HALF
PAD = KEPT + 64
BLK = 128
BIG = 384


def dot(left, right):
    return jnp.dot(left, right, preferred_element_type=F32)


def dot_last(left, right):
    return lax.dot_general(left, right, (((1,), (1,)), ((), ())), preferred_element_type=F32)


def iota(shape, dim):
    return lax.broadcasted_iota(jnp.int32, shape, dim)


def loop(lo, hi, step, unroll=1):
    def run(index, carry):
        step(index)
        return carry

    lax.fori_loop(lo, hi, run, 0, unroll=unroll)


def kernel(
    gains, order, count_v, count_s, q_hbm, k_hbm, v_hbm, g_hbm,
    outs, gain_out,
    xs, send_qk, send_vg, recv_qk, recv_vg, send_ov, send_dd, recv_ov, recv_dd,
    pack_a, pack_b, unpack, hot_a, hot_b, place_a, place_b,
    prob, prob_b, ds_b, qn, kn, vv, gg, uq, uk, iq, ik, qn_t, gg_t,
    y_o, y_dv, y_dq, y_dk, gsend, gbuf, hsend, hbuf, total, starts,
    met, rowed, in_sem, fs, fr, bs, br, dds, ddr, gs, gr,
):
    me = lax.axis_index("ctx")
    dp = lax.axis_index("dp")
    own_sample = me // HEADS
    scale = HD ** (-0.5)

    def ahead(k):
        return lax.rem(me + k, DEV)

    def behind(k):
        return lax.rem(me + DEV - k, DEV)

    def pairs(lo, hi, step):
        def both(k):
            step(k)
            step(DEV - k)

        loop(lo, hi, both)

    def spread(step):
        pairs(1, DEV // 2, step)
        step(DEV // 2)

    y, x = me // NX, lax.rem(me, NX)

    def partner(j, i):
        return lax.rem(y + j, NY) * NX + lax.rem(x + i, NX)

    def step_to(j, i):
        return lax.rem(partner(j, i) - me + DEV, DEV)

    is_hub = me == 0
    barrier = pltpu.get_barrier_semaphore()

    def greet(device):
        @pl.when(device != 0)
        def _():
            pl.semaphore_signal(
                barrier, inc=1, device_id={"ctx": device}, device_id_type=MESH
            )

    loop(1, NY, lambda j: greet(partner(j, 0)))
    loop(1, NX, lambda i: greet(partner(0, i)))

    @pl.when(is_hub)
    def _():
        loop(1, DP, lambda k: pl.semaphore_signal(
            barrier, inc=1, device_id={"dp": lax.rem(dp + k, DP)}, device_id_type=MESH))

    loads = [
        pltpu.make_async_copy(ref, xs.at[i], in_sem.at[i])
        for i, ref in enumerate((q_hbm, k_hbm, v_hbm, g_hbm))
    ]
    for load in loads:
        load.start()

    row, slot = iota((MSG, TS), 0), iota((MSG, TS), 1)
    pick_a = ((row == slot) & (row < 54)).astype(F32).astype(BF)
    pick_b = (
        ((row >= HALF) & (slot == row - HALF)) | ((row >= 56) & (row < 62) & (slot == row - 8))
    ).astype(F32).astype(BF)
    for s in range(2):
        tokens = order[s, pl.ds(me, 1), :]
        own_count = count_s[s, me]
        chosen = ((iota((TS, TS), 0) == tokens) & (iota((TS, TS), 1) < own_count))
        chosen = chosen.astype(F32).astype(BF)
        pack_a[s] = dot_last(pick_a, chosen).astype(BF)
        pack_b[s] = dot_last(pick_b, chosen).astype(BF)
        unpack[s, 0:TS] = dot_last(chosen, pick_a).astype(BF)
        unpack[s, TS : 2 * TS] = dot_last(chosen, pick_b).astype(BF)

    for load in loads:
        load.wait()

    def packed(k):
        pair = ahead(k)
        s = pair // HEADS
        first = jnp.concatenate([xs[0, pair], xs[2, pair]], axis=1)
        second = jnp.concatenate([xs[1, pair], xs[3, pair]], axis=1)
        rows = (dot(pack_a[s], first) + dot(pack_b[s], second)).astype(BF)
        return rows[:, :HD], rows[:, HD:]

    @pl.when(jnp.logical_not(is_hub))
    def _():
        pl.semaphore_wait(barrier, NY - 1 + NX - 1)

        @pl.when(x * y == 0)
        def _():
            pl.semaphore_signal(met, inc=1, device_id={"ctx": 0}, device_id_type=MESH)

    @pl.when(is_hub)
    def _():
        pl.semaphore_wait(met, NY - 1 + NX - 1)

    loop(1, NY, lambda j: pl.semaphore_signal(
        rowed, inc=1, device_id={"ctx": partner(j, 0)}, device_id_type=MESH))

    def remote(src, dst, send_sem, recv_sem, peer):
        return pltpu.make_async_remote_copy(
            src_ref=src, dst_ref=dst, send_sem=send_sem, recv_sem=recv_sem,
            device_id={"ctx": peer}, device_id_type=MESH)

    def part(src, dst, which, lo, size, sems, semr, peer):
        rows = pl.ds(lo, size)
        return remote(
            src.at[which, rows], dst.at[which, rows], sems, semr, peer
        )

    every = pl.ds(1, DEV - 1)

    def pack(*steps):
        rows = [packed(k) for k in steps]
        for k, (first, second) in zip(steps, rows, strict=True):
            send_qk[k], send_vg[k] = first, second
        for k in steps:
            part(send_qk, recv_qk, k, 0, MSG, fs.at[0], fr.at[0], ahead(k)).start()

    loop(1, NY // 2, lambda j: pack(step_to(j, 0), step_to(NY - j, 0)))
    pack(step_to(0, 1), step_to(0, 3))
    pack(step_to(NY // 2, 0), step_to(0, 2))
    pl.semaphore_wait(rowed, NY - 1)

    def pack_others(n):
        j, i = 1 + n // (NX - 1), 1 + lax.rem(n, NX - 1)
        pack(step_to(j, i), step_to(NY - j, i))

    loop(0, (NY // 2 - 1) * (NX - 1), pack_others)
    loop(1, NX, lambda i: pack(step_to(NY // 2, i)))
    spread(lambda k: part(
        send_vg, recv_vg, k, 0, HALF, fs.at[1], fr.at[1], ahead(k)).start())
    spread(lambda k: part(
        send_vg, recv_vg, k, HALF, MAIN, fs.at[2], fr.at[2], ahead(k)).start())
    all_qk = part(send_qk, recv_qk, every, 0, MSG, fs.at[0], fr.at[0], ahead(1))
    all_v = part(send_vg, recv_vg, every, 0, HALF, fs.at[1], fr.at[1], ahead(1))
    all_g = part(send_vg, recv_vg, every, HALF, MAIN, fs.at[2], fr.at[2], ahead(1))

    recv_qk[0], recv_vg[0] = packed(0)

    def add_start(c, total):
        starts[c] = total
        return total + count_s[own_sample, c]

    lax.fori_loop(0, DEV, add_start, jnp.int32(0))
    counts = count_v[pl.ds(own_sample, 1), :].astype(F32)
    upto = (iota((DEV, DEV), 0) <= iota((DEV, DEV), 1)).astype(F32).astype(BF)
    ends = dot(jnp.broadcast_to(counts, (8, DEV)).astype(BF), upto)[0:1, :]
    ranks = iota((KEPT, DEV), 0).astype(F32)
    past = ends <= ranks
    shard = jnp.sum(jnp.where(past, 1.0, 0.0), axis=1, keepdims=True)
    start = jnp.sum(jnp.where(past, counts, 0.0), axis=1, keepdims=True)
    within = iota((KEPT, 1), 0).astype(F32) - start
    place = me.astype(F32) - shard
    place = jnp.where(place < 0.0, place + DEV, place) * HALF
    at_a = (place + within).astype(jnp.int32)
    at_b = (place + jnp.where(within < MAIN, within + 16.0, within - 40.0)).astype(jnp.int32)
    place_a[...] = jnp.broadcast_to(at_a, (KEPT, HD))
    place_b[...] = jnp.broadcast_to(at_b, (KEPT, HD))

    def fill(b):
        rows = pl.ds(pl.multiple_of(b * BLK, BLK), BLK)
        lane = iota((BLK, HD), 1)
        for where, hot in ((place_a, hot_a), (place_b, hot_b)):
            at = where[rows] - lane
            for n in range(WIDE // HD):
                hot[rows, n * HD : (n + 1) * HD] = (at == n * HD).astype(F32).astype(BF)

    loop(0, KEPT // BLK, fill)
    for y in (y_o, y_dv, y_dq, y_dk):
        y[KEPT:PAD] = jnp.zeros((PAD - KEPT, HD), F32)

    def big(b):
        return pl.ds(pl.multiple_of(b * BIG, BIG), BIG)

    def gather(hot, rows, recv, lo):
        return dot(hot[rows], recv[:, lo : lo + HALF].reshape(WIDE, HD))

    all_qk.wait_recv()

    def norms(b):
        rows = big(b)
        for hot, lo, unit_ref, inv_ref, norm_ref, i in (
            (hot_a, 0, uq, iq, qn, 0),
            (hot_b, MAIN, uk, ik, kn, 1),
        ):
            x = gather(hot, rows, recv_qk, lo)
            inv = lax.rsqrt(jnp.mean(x * x, axis=-1, keepdims=True) + EPS)
            unit = x * inv
            unit_ref[rows] = unit
            inv_ref[rows] = jnp.broadcast_to(inv, (BIG, HD))
            norm_ref[rows] = (unit * gains[i : i + 1, :]).astype(BF)

    loop(0, KEPT // BIG, norms)
    qn_t[...] = jnp.transpose(qn[...].astype(F32)).astype(BF)

    def softmax(b):
        rows = pl.ds(pl.multiple_of(b * BLK, BLK), BLK)
        scores = dot_last(qn[rows], kn[...]) * scale
        peak = jnp.max(scores, axis=-1, keepdims=True)
        expo = jnp.exp(scores - peak)
        p = expo / jnp.sum(expo, axis=-1, keepdims=True)
        prob[rows] = p
        prob_b[rows] = p.astype(BF)

    loop(0, KEPT // BLK, softmax)

    all_v.wait_recv()

    def attend(b):
        vv[big(b)] = gather(hot_a, big(b), recv_vg, 0).astype(BF)

    loop(0, KEPT // BIG, attend)

    def attend2(b):
        y_o[big(b)] = dot(prob_b[big(b)], vv[...])

    loop(0, KEPT // BIG, attend2)

    def main_rows(y, k):
        return y[pl.ds(starts[behind(k)], MAIN), :].astype(BF)

    def tail_rows(y, z, k):
        at = pl.ds(starts[behind(k)] + MAIN, 8)
        return jnp.concatenate([y[at, :], z[at, :]], axis=0).astype(BF)

    recv_ov[0, 0:MAIN] = main_rows(y_o, 0)

    def out_main(k):
        send_ov[k, 0:MAIN] = main_rows(y_o, k)

    loop(1, DEV, out_main)
    all_g.wait_send()
    spread(lambda k: part(
        send_ov, recv_ov, k, 0, MAIN, bs.at[0], br.at[0], behind(k)).start())
    all_o = part(send_ov, recv_ov, every, 0, MAIN, bs.at[0], br.at[0], behind(1))

    all_g.wait_recv()

    def cotangents(b):
        gg[big(b)] = gather(hot_b, big(b), recv_vg, MAIN).astype(BF)

    loop(0, KEPT // BIG, cotangents)
    gg_t[...] = jnp.transpose(gg[...].astype(F32)).astype(BF)

    def column(b):
        return pl.ds(pl.multiple_of(b * BIG, BIG), BIG)

    def value_back(b):
        y_dv[big(b)] = jnp.transpose(dot(gg_t[...], prob_b[:, column(b)]))

    loop(0, KEPT // BIG, value_back)
    recv_ov[0, MAIN:HALF] = tail_rows(y_o, y_dv, 0)
    recv_ov[0, HALF:MSG] = main_rows(y_dv, 0)

    def value_main(k):
        send_ov[k, MAIN:HALF] = tail_rows(y_o, y_dv, k)
        send_ov[k, HALF:MSG] = main_rows(y_dv, k)
        part(send_ov, recv_ov, k, MAIN, HALF, bs.at[1], br.at[1], behind(k)).start()

    spread(value_main)
    all_dv = part(send_ov, recv_ov, every, MAIN, HALF, bs.at[1], br.at[1], behind(1))

    def score_back(b):
        rows = pl.ds(pl.multiple_of(b * BLK, BLK), BLK)
        dprob = dot_last(gg[rows], vv[...])
        p = prob[rows]
        delta = jnp.sum(p * dprob, axis=-1, keepdims=True)
        ds_b[rows] = (p * (dprob - delta)).astype(BF)

    loop(0, KEPT // BLK, score_back)

    def norm_back(grad, rows, unit_ref, inv_ref, i, y):
        unit = unit_ref[rows]
        tangent = grad * gains[i : i + 1, :]
        y[rows] = inv_ref[rows] * (
            tangent - unit * jnp.mean(tangent * unit, axis=-1, keepdims=True)
        )
        gsend[i : i + 1, :] += jnp.sum(grad * unit, axis=0, keepdims=True)

    gsend[...] = jnp.zeros_like(gsend)

    def query_back(b):
        grad = dot(ds_b[big(b)], kn[...]) * scale
        norm_back(grad, big(b), uq, iq, 0, y_dq)

    loop(0, KEPT // BIG, query_back)

    def key_back(b):
        grad = jnp.transpose(dot(qn_t[...], ds_b[:, column(b)])) * scale
        norm_back(grad, big(b), uk, ik, 1, y_dk)

    loop(0, KEPT // BIG, key_back)

    to_hub = remote(gsend, gbuf.at[me], gs.at[0], gr.at[0], 0)
    from_devs = remote(gbuf.at[every], gbuf.at[every], gs.at[0], gr.at[0], 0)
    others = pl.ds(1, DP - 1)

    def to_group(k):
        return remote(total.at[0], total.at[1], gs.at[2], gr.at[2], ahead(k))

    def between(src, dst, k):
        return pltpu.make_async_remote_copy(
            src_ref=src, dst_ref=dst, send_sem=gs.at[1], recv_sem=gr.at[1],
            device_id={"dp": lax.rem(dp + k, DP)}, device_id_type=MESH)

    @pl.when(jnp.logical_not(is_hub))
    def _():
        to_hub.start()

    def grad_rows(k):
        return main_rows(y_dq, k), tail_rows(y_dq, y_dk, k), main_rows(y_dk, k)

    recv_dd[0, 0:MAIN], recv_dd[0, MAIN:HALF], recv_dd[0, HALF:MSG] = grad_rows(0)

    def back_dd(k):
        return part(send_dd, recv_dd, k, 0, MSG, dds, ddr.at[k], behind(k))

    def grad_main(k):
        send_dd[k, 0:MAIN], send_dd[k, MAIN:HALF], send_dd[k, HALF:MSG] = grad_rows(k)
        back_dd(k).start()

    spread(grad_main)

    @pl.when(is_hub)
    def _():
        gbuf[0] = gsend[...]
        from_devs.wait_recv()
        hsend[...] = lax.fori_loop(
            0, DEV, lambda c, acc: acc + gbuf[c], jnp.zeros((8, HD), F32)
        )
        hbuf[0] = hsend[...]
        pl.semaphore_wait(barrier, DP - 1)
        loop(1, DP, lambda k: between(hsend, hbuf.at[k], k).start())

    all_dd = part(send_dd, recv_dd, every, 0, MSG, dds, ddr.at[0], behind(1))

    all_o.wait_recv()
    all_dv.wait_recv()

    def home(k, recv, first, second):
        pair = ahead(k)
        rows = dot(unpack[pair // HEADS], recv[k]).astype(BF)
        outs[first, pair] = rows[:TS]
        outs[second, pair] = rows[TS:]

    loop(0, DEV, lambda k: home(k, recv_ov, 0, 3))
    @pl.when(is_hub)
    def _():
        between(hbuf.at[others], hbuf.at[others], 1).wait_recv()
        total[0] = lax.fori_loop(
            0, DP, lambda c, acc: acc + hbuf[lax.rem(dp + DP - c, DP)], jnp.zeros((8, HD), F32)
        )
        total[1] = total[0]
        loop(1, DEV, lambda k: to_group(k).start())

    home(0, recv_dd, 1, 2)

    def last(k):
        back_dd(k).wait_recv()
        home(k, recv_dd, 1, 2)

    spread(last)

    @pl.when(is_hub)
    def _():
        between(hbuf.at[others], hbuf.at[others], 1).wait_send()
        loop(1, DEV, lambda k: to_group(k).wait_send())

    @pl.when(jnp.logical_not(is_hub))
    def _():
        to_hub.wait_send()
        to_group(1).wait_recv()

    gain_out[...] = total[1, 0:2]
    all_qk.wait_send()
    all_v.wait_send()
    all_o.wait_send()
    all_dv.wait_send()
    all_dd.wait_send()


def deal(merged, gain, o_out, dq_out, dk_out, dv_out, gain_out, sem):
    copies = [
        pltpu.make_async_copy(merged.at[i, rows], ref.at[rows], sem.at[i, n])
        for n in range(4)
        for rows in (pl.ds(n * (DEV // 4), DEV // 4),)
        for i, ref in enumerate((o_out, dq_out, dk_out, dv_out))
    ]
    for copy in copies:
        copy.start()
    gain_out[...] = gain[...]
    for copy in copies:
        copy.wait()


def body(queries, keys, values, out_grad, gains, keep_order, keep_count):
    pairs = [x.reshape(DEV, TS, HD) for x in (queries, keys, values, out_grad)]
    vmem = pl.BlockSpec(memory_space=pltpu.VMEM)
    smem = pl.BlockSpec(memory_space=pltpu.SMEM)
    hbm = pl.BlockSpec(memory_space=pl.ANY)
    message = pltpu.VMEM((DEV, MSG, HD), BF)
    rows_b, rows_f = pltpu.VMEM((KEPT, HD), BF), pltpu.VMEM((KEPT, HD), F32)
    result = pltpu.VMEM((PAD, HD), F32)
    place = pltpu.VMEM((KEPT, HD), jnp.int32)
    hot = pltpu.VMEM((KEPT, WIDE), BF)
    square_f, square_b = pltpu.VMEM((KEPT, KEPT), F32), pltpu.VMEM((KEPT, KEPT), BF)
    turned = pltpu.VMEM((HD, KEPT), BF)
    dma = pltpu.SemaphoreType.DMA
    out = jax.ShapeDtypeStruct((DEV, TS, HD), BF)
    gain_shape = jax.ShapeDtypeStruct((2, HD), F32)
    merged, gain = pl.pallas_call(
        kernel,
        out_shape=[pltpu.VMEM((4, DEV, TS, HD), BF), pltpu.VMEM((2, HD), F32)],
        in_specs=[vmem, vmem, vmem, smem] + [hbm] * 4,
        out_specs=[vmem, vmem],
        scratch_shapes=[pltpu.VMEM((4, DEV, TS, HD), BF)]
        + [message] * 8
        + [pltpu.VMEM((2, MSG, TS), BF)] * 2
        + [pltpu.VMEM((2, 2 * TS, MSG), BF)]
        + [hot] * 2
        + [place] * 2
        + [square_f, square_b, square_b]
        + [rows_b] * 4
        + [rows_f] * 4
        + [turned] * 2
        + [result] * 4
        + [pltpu.VMEM((8, HD), F32), pltpu.VMEM((DEV, 8, HD), F32)]
        + [pltpu.VMEM((8, HD), F32), pltpu.VMEM((DP, 8, HD), F32)]
        + [pltpu.VMEM((2, 8, HD), F32)]
        + [pltpu.SMEM((DEV,), jnp.int32)]
        + [pltpu.SemaphoreType.REGULAR] * 2
        + [dma((4,)), dma((3,)), dma((3,)), dma((2,)), dma((2,))]
        + [dma, dma((DEV,)), dma((3,)), dma((3,))],
        compiler_params=pltpu.CompilerParams(
            collective_id=0, has_side_effects=True, vmem_limit_bytes=60 * 1024 * 1024
        ),
    )(gains, keep_order, keep_count, keep_count, *pairs)
    results = pl.pallas_call(
        deal,
        out_shape=[out] * 4 + [gain_shape],
        in_specs=[vmem, vmem],
        out_specs=[hbm] * 4 + [vmem],
        scratch_shapes=[dma((4, 4))],
        compiler_params=pltpu.CompilerParams(vmem_limit_bytes=8 * 1024 * 1024),
    )(merged, gain)
    shape = queries.shape
    return tuple(r.reshape(shape) for r in results[:4]) + (results[4],)


def solution(mesh):
    rows = P("dp", None, "ctx", None)
    return jax.shard_map(
        body,
        mesh=mesh,
        in_specs=(rows, rows, rows, rows, P(), P("dp", None, None), P("dp", None)),
        out_specs=(rows, rows, rows, rows, P()),
        check_vma=False,
    )
```

```python
import jax
import jax.numpy as jnp
from jax import lax
from jax.experimental import pallas as pl
from jax.experimental.pallas import tpu as pltpu
from jax.sharding import PartitionSpec as P

EPS = 1e-06
MESH = pl.DeviceIdType.MESH
BF = jnp.bfloat16
F32 = jnp.float32

DEV = 32
NY, NX = 8, 4
DP = 16
HEADS = 16
TS = 72
HD = 128
KEPT = 1152
MSG = 112
MAIN = 48
HALF = 64
WIDE = DEV * HALF
PAD = KEPT + 64
BLK = 128
BIG = 384


def dot(left, right):
    return jnp.dot(left, right, preferred_element_type=F32)


def dot_last(left, right):
    return lax.dot_general(left, right, (((1,), (1,)), ((), ())), preferred_element_type=F32)


def iota(shape, dim):
    return lax.broadcasted_iota(jnp.int32, shape, dim)


def loop(lo, hi, step, unroll=1):
    def run(index, carry):
        step(index)
        return carry

    lax.fori_loop(lo, hi, run, 0, unroll=unroll)


def kernel(
    gains_hbm, order_hbm, count_hbm, q_hbm, k_hbm, v_hbm, g_hbm,
    outs, gain_out,
    gains, order, count_v, count_s, xs, send_qk, send_vg, recv_qk, recv_vg, send_ov, send_dd, recv_ov, recv_dd,
    pack_a, pack_b, unpack, hot_a, hot_b, place_a, place_b,
    prob, prob_b, ds_b, qn, kn, vv, gg, uq, uk, iq, ik, qn_t, gg_t,
    y_o, y_dv, y_dq, y_dk, gsend, gbuf, hsend, hbuf, total, starts,
    met, rowed, in_sem, fs, fr, bs, br, dds, ddr, gs, gr,
):
    me = lax.axis_index("ctx")
    dp = lax.axis_index("dp")
    own_sample = me // HEADS
    scale = HD ** (-0.5)

    def ahead(k):
        return lax.rem(me + k, DEV)

    def behind(k):
        return lax.rem(me + DEV - k, DEV)

    def pairs(lo, hi, step):
        def both(k):
            step(k)
            step(DEV - k)

        loop(lo, hi, both)

    def spread(step):
        pairs(1, DEV // 2, step)
        step(DEV // 2)

    y, x = me // NX, lax.rem(me, NX)

    def partner(j, i):
        return lax.rem(y + j, NY) * NX + lax.rem(x + i, NX)

    def step_to(j, i):
        return lax.rem(partner(j, i) - me + DEV, DEV)

    is_hub = me == 0
    barrier = pltpu.get_barrier_semaphore()

    def greet(device):
        @pl.when(device != 0)
        def _():
            pl.semaphore_signal(
                barrier, inc=1, device_id={"ctx": device}, device_id_type=MESH
            )

    loop(1, NY, lambda j: greet(partner(j, 0)))
    loop(1, NX, lambda i: greet(partner(0, i)))

    @pl.when(is_hub)
    def _():
        loop(1, DP, lambda k: pl.semaphore_signal(
            barrier, inc=1, device_id={"dp": lax.rem(dp + k, DP)}, device_id_type=MESH))

    small = [
        pltpu.make_async_copy(ref, into, in_sem.at[4 + i])
        for i, (ref, into) in enumerate(
            ((order_hbm, order), (count_hbm, count_s), (count_hbm, count_v), (gains_hbm, gains))
        )
    ]
    loads = [
        pltpu.make_async_copy(ref, xs.at[i], in_sem.at[i])
        for i, ref in enumerate((q_hbm, k_hbm, v_hbm, g_hbm))
    ]
    for load in small + loads:
        load.start()
    for load in small:
        load.wait()

    row, slot = iota((MSG, TS), 0), iota((MSG, TS), 1)
    pick_a = ((row == slot) & (row < 54)).astype(F32).astype(BF)
    pick_b = (
        ((row >= HALF) & (slot == row - HALF)) | ((row >= 56) & (row < 62) & (slot == row - 8))
    ).astype(F32).astype(BF)
    for s in range(2):
        tokens = order[s, pl.ds(me, 1), :]
        own_count = count_s[s, me]
        chosen = ((iota((TS, TS), 0) == tokens) & (iota((TS, TS), 1) < own_count))
        chosen = chosen.astype(F32).astype(BF)
        pack_a[s] = dot_last(pick_a, chosen).astype(BF)
        pack_b[s] = dot_last(pick_b, chosen).astype(BF)
        unpack[s, 0:TS] = dot_last(chosen, pick_a).astype(BF)
        unpack[s, TS : 2 * TS] = dot_last(chosen, pick_b).astype(BF)

    for load in loads:
        load.wait()

    def packed(k):
        pair = ahead(k)
        s = pair // HEADS
        first = jnp.concatenate([xs[0, pair], xs[2, pair]], axis=1)
        second = jnp.concatenate([xs[1, pair], xs[3, pair]], axis=1)
        rows = (dot(pack_a[s], first) + dot(pack_b[s], second)).astype(BF)
        return rows[:, :HD], rows[:, HD:]

    @pl.when(jnp.logical_not(is_hub))
    def _():
        pl.semaphore_wait(barrier, NY - 1 + NX - 1)

        @pl.when(x * y == 0)
        def _():
            pl.semaphore_signal(met, inc=1, device_id={"ctx": 0}, device_id_type=MESH)

    @pl.when(is_hub)
    def _():
        pl.semaphore_wait(met, NY - 1 + NX - 1)

    loop(1, NY, lambda j: pl.semaphore_signal(
        rowed, inc=1, device_id={"ctx": partner(j, 0)}, device_id_type=MESH))

    def remote(src, dst, send_sem, recv_sem, peer):
        return pltpu.make_async_remote_copy(
            src_ref=src, dst_ref=dst, send_sem=send_sem, recv_sem=recv_sem,
            device_id={"ctx": peer}, device_id_type=MESH)

    def part(src, dst, which, lo, size, sems, semr, peer):
        rows = pl.ds(lo, size)
        return remote(
            src.at[which, rows], dst.at[which, rows], sems, semr, peer
        )

    every = pl.ds(1, DEV - 1)

    def pack(*steps):
        rows = [packed(k) for k in steps]
        for k, (first, second) in zip(steps, rows, strict=True):
            send_qk[k], send_vg[k] = first, second
        for k in steps:
            part(send_qk, recv_qk, k, 0, MSG, fs.at[0], fr.at[0], ahead(k)).start()

    loop(1, NY // 2, lambda j: pack(step_to(j, 0), step_to(NY - j, 0)))
    pack(step_to(0, 1), step_to(0, 3))
    pack(step_to(NY // 2, 0), step_to(0, 2))
    pl.semaphore_wait(rowed, NY - 1)

    def pack_others(n):
        j, i = 1 + n // (NX - 1), 1 + lax.rem(n, NX - 1)
        pack(step_to(j, i), step_to(NY - j, i))

    loop(0, (NY // 2 - 1) * (NX - 1), pack_others)
    loop(1, NX, lambda i: pack(step_to(NY // 2, i)))
    spread(lambda k: part(
        send_vg, recv_vg, k, 0, HALF, fs.at[1], fr.at[1], ahead(k)).start())
    spread(lambda k: part(
        send_vg, recv_vg, k, HALF, MAIN, fs.at[2], fr.at[2], ahead(k)).start())
    all_qk = part(send_qk, recv_qk, every, 0, MSG, fs.at[0], fr.at[0], ahead(1))
    all_v = part(send_vg, recv_vg, every, 0, HALF, fs.at[1], fr.at[1], ahead(1))
    all_g = part(send_vg, recv_vg, every, HALF, MAIN, fs.at[2], fr.at[2], ahead(1))

    recv_qk[0], recv_vg[0] = packed(0)

    def add_start(c, total):
        starts[c] = total
        return total + count_s[own_sample, c]

    lax.fori_loop(0, DEV, add_start, jnp.int32(0))
    counts = count_v[pl.ds(own_sample, 1), :].astype(F32)
    upto = (iota((DEV, DEV), 0) <= iota((DEV, DEV), 1)).astype(F32).astype(BF)
    ends = dot(jnp.broadcast_to(counts, (8, DEV)).astype(BF), upto)[0:1, :]
    ranks = iota((KEPT, DEV), 0).astype(F32)
    past = ends <= ranks
    shard = jnp.sum(jnp.where(past, 1.0, 0.0), axis=1, keepdims=True)
    start = jnp.sum(jnp.where(past, counts, 0.0), axis=1, keepdims=True)
    within = iota((KEPT, 1), 0).astype(F32) - start
    place = me.astype(F32) - shard
    place = jnp.where(place < 0.0, place + DEV, place) * HALF
    at_a = (place + within).astype(jnp.int32)
    at_b = (place + jnp.where(within < MAIN, within + 16.0, within - 40.0)).astype(jnp.int32)
    place_a[...] = jnp.broadcast_to(at_a, (KEPT, HD))
    place_b[...] = jnp.broadcast_to(at_b, (KEPT, HD))

    def fill(b):
        rows = pl.ds(pl.multiple_of(b * BLK, BLK), BLK)
        lane = iota((BLK, HD), 1)
        for where, hot in ((place_a, hot_a), (place_b, hot_b)):
            at = where[rows] - lane
            for n in range(WIDE // HD):
                hot[rows, n * HD : (n + 1) * HD] = (at == n * HD).astype(F32).astype(BF)

    loop(0, KEPT // BLK, fill)
    for y in (y_o, y_dv, y_dq, y_dk):
        y[KEPT:PAD] = jnp.zeros((PAD - KEPT, HD), F32)

    def big(b):
        return pl.ds(pl.multiple_of(b * BIG, BIG), BIG)

    def gather(hot, rows, recv, lo):
        return dot(hot[rows], recv[:, lo : lo + HALF].reshape(WIDE, HD))

    all_qk.wait_recv()

    def norms(b):
        rows = big(b)
        for hot, lo, unit_ref, inv_ref, norm_ref, i in (
            (hot_a, 0, uq, iq, qn, 0),
            (hot_b, MAIN, uk, ik, kn, 1),
        ):
            x = gather(hot, rows, recv_qk, lo)
            inv = lax.rsqrt(jnp.mean(x * x, axis=-1, keepdims=True) + EPS)
            unit = x * inv
            unit_ref[rows] = unit
            inv_ref[rows] = jnp.broadcast_to(inv, (BIG, HD))
            norm_ref[rows] = (unit * gains[i : i + 1, :]).astype(BF)

    loop(0, KEPT // BIG, norms)
    qn_t[...] = jnp.transpose(qn[...].astype(F32)).astype(BF)

    def softmax(b):
        rows = pl.ds(pl.multiple_of(b * BLK, BLK), BLK)
        scores = dot_last(qn[rows], kn[...]) * scale
        peak = jnp.max(scores, axis=-1, keepdims=True)
        expo = jnp.exp(scores - peak)
        p = expo / jnp.sum(expo, axis=-1, keepdims=True)
        prob[rows] = p
        prob_b[rows] = p.astype(BF)

    loop(0, KEPT // BLK, softmax)

    all_v.wait_recv()

    def attend(b):
        vv[big(b)] = gather(hot_a, big(b), recv_vg, 0).astype(BF)

    loop(0, KEPT // BIG, attend)

    def attend2(b):
        y_o[big(b)] = dot(prob_b[big(b)], vv[...])

    loop(0, KEPT // BIG, attend2)

    def main_rows(y, k):
        return y[pl.ds(starts[behind(k)], MAIN), :].astype(BF)

    def tail_rows(y, z, k):
        at = pl.ds(starts[behind(k)] + MAIN, 8)
        return jnp.concatenate([y[at, :], z[at, :]], axis=0).astype(BF)

    recv_ov[0, 0:MAIN] = main_rows(y_o, 0)

    def out_main(k):
        send_ov[k, 0:MAIN] = main_rows(y_o, k)

    loop(1, DEV, out_main)
    all_g.wait_send()
    spread(lambda k: part(
        send_ov, recv_ov, k, 0, MAIN, bs.at[0], br.at[0], behind(k)).start())
    all_o = part(send_ov, recv_ov, every, 0, MAIN, bs.at[0], br.at[0], behind(1))

    all_g.wait_recv()

    def cotangents(b):
        gg[big(b)] = gather(hot_b, big(b), recv_vg, MAIN).astype(BF)

    loop(0, KEPT // BIG, cotangents)
    gg_t[...] = jnp.transpose(gg[...].astype(F32)).astype(BF)

    def column(b):
        return pl.ds(pl.multiple_of(b * BIG, BIG), BIG)

    def value_back(b):
        y_dv[big(b)] = jnp.transpose(dot(gg_t[...], prob_b[:, column(b)]))

    loop(0, KEPT // BIG, value_back)
    recv_ov[0, MAIN:HALF] = tail_rows(y_o, y_dv, 0)
    recv_ov[0, HALF:MSG] = main_rows(y_dv, 0)

    def value_main(k):
        send_ov[k, MAIN:HALF] = tail_rows(y_o, y_dv, k)
        send_ov[k, HALF:MSG] = main_rows(y_dv, k)
        part(send_ov, recv_ov, k, MAIN, HALF, bs.at[1], br.at[1], behind(k)).start()

    spread(value_main)
    all_dv = part(send_ov, recv_ov, every, MAIN, HALF, bs.at[1], br.at[1], behind(1))

    def score_back(b):
        rows = pl.ds(pl.multiple_of(b * BLK, BLK), BLK)
        dprob = dot_last(gg[rows], vv[...])
        p = prob[rows]
        delta = jnp.sum(p * dprob, axis=-1, keepdims=True)
        ds_b[rows] = (p * (dprob - delta)).astype(BF)

    loop(0, KEPT // BLK, score_back)

    def norm_back(grad, rows, unit_ref, inv_ref, i, y):
        unit = unit_ref[rows]
        tangent = grad * gains[i : i + 1, :]
        y[rows] = inv_ref[rows] * (
            tangent - unit * jnp.mean(tangent * unit, axis=-1, keepdims=True)
        )
        gsend[i : i + 1, :] += jnp.sum(grad * unit, axis=0, keepdims=True)

    gsend[...] = jnp.zeros_like(gsend)

    def query_back(b):
        grad = dot(ds_b[big(b)], kn[...]) * scale
        norm_back(grad, big(b), uq, iq, 0, y_dq)

    loop(0, KEPT // BIG, query_back)

    def key_back(b):
        grad = jnp.transpose(dot(qn_t[...], ds_b[:, column(b)])) * scale
        norm_back(grad, big(b), uk, ik, 1, y_dk)

    loop(0, KEPT // BIG, key_back)

    to_hub = remote(gsend, gbuf.at[me], gs.at[0], gr.at[0], 0)
    from_devs = remote(gbuf.at[every], gbuf.at[every], gs.at[0], gr.at[0], 0)
    others = pl.ds(1, DP - 1)

    def to_group(k):
        return remote(total.at[0], total.at[1], gs.at[2], gr.at[2], ahead(k))

    def between(src, dst, k):
        return pltpu.make_async_remote_copy(
            src_ref=src, dst_ref=dst, send_sem=gs.at[1], recv_sem=gr.at[1],
            device_id={"dp": lax.rem(dp + k, DP)}, device_id_type=MESH)

    @pl.when(jnp.logical_not(is_hub))
    def _():
        to_hub.start()

    def grad_rows(k):
        return main_rows(y_dq, k), tail_rows(y_dq, y_dk, k), main_rows(y_dk, k)

    recv_dd[0, 0:MAIN], recv_dd[0, MAIN:HALF], recv_dd[0, HALF:MSG] = grad_rows(0)

    def back_dd(k):
        return part(send_dd, recv_dd, k, 0, MSG, dds, ddr.at[k], behind(k))

    def grad_main(k):
        send_dd[k, 0:MAIN], send_dd[k, MAIN:HALF], send_dd[k, HALF:MSG] = grad_rows(k)
        back_dd(k).start()

    spread(grad_main)

    @pl.when(is_hub)
    def _():
        gbuf[0] = gsend[...]
        from_devs.wait_recv()
        hsend[...] = lax.fori_loop(
            0, DEV, lambda c, acc: acc + gbuf[c], jnp.zeros((8, HD), F32)
        )
        hbuf[0] = hsend[...]
        pl.semaphore_wait(barrier, DP - 1)
        loop(1, DP, lambda k: between(hsend, hbuf.at[k], k).start())

    all_dd = part(send_dd, recv_dd, every, 0, MSG, dds, ddr.at[0], behind(1))

    all_o.wait_recv()
    all_dv.wait_recv()

    def home(k, recv, first, second):
        pair = ahead(k)
        rows = dot(unpack[pair // HEADS], recv[k]).astype(BF)
        outs[first, pair] = rows[:TS]
        outs[second, pair] = rows[TS:]

    loop(0, DEV, lambda k: home(k, recv_ov, 0, 3))
    @pl.when(is_hub)
    def _():
        between(hbuf.at[others], hbuf.at[others], 1).wait_recv()
        total[0] = lax.fori_loop(
            0, DP, lambda c, acc: acc + hbuf[lax.rem(dp + DP - c, DP)], jnp.zeros((8, HD), F32)
        )
        total[1] = total[0]
        loop(1, DEV, lambda k: to_group(k).start())

    home(0, recv_dd, 1, 2)

    def last(k):
        back_dd(k).wait_recv()
        home(k, recv_dd, 1, 2)

    spread(last)

    @pl.when(is_hub)
    def _():
        between(hbuf.at[others], hbuf.at[others], 1).wait_send()
        loop(1, DEV, lambda k: to_group(k).wait_send())

    @pl.when(jnp.logical_not(is_hub))
    def _():
        to_hub.wait_send()
        to_group(1).wait_recv()

    gain_out[...] = total[1, 0:2]
    all_qk.wait_send()
    all_v.wait_send()
    all_o.wait_send()
    all_dv.wait_send()
    all_dd.wait_send()


def deal(merged, gain, o_out, dq_out, dk_out, dv_out, gain_out, sem):
    copies = [
        pltpu.make_async_copy(merged.at[i, rows], ref.at[rows], sem.at[i, n])
        for n in range(4)
        for rows in (pl.ds(n * (DEV // 4), DEV // 4),)
        for i, ref in enumerate((o_out, dq_out, dk_out, dv_out))
    ]
    for copy in copies:
        copy.start()
    gain_out[...] = gain[...]
    for copy in copies:
        copy.wait()


def body(queries, keys, values, out_grad, gains, keep_order, keep_count):
    pairs = [x.reshape(DEV, TS, HD) for x in (queries, keys, values, out_grad)]
    vmem = pl.BlockSpec(memory_space=pltpu.VMEM)
    hbm = pl.BlockSpec(memory_space=pl.ANY)
    message = pltpu.VMEM((DEV, MSG, HD), BF)
    rows_b, rows_f = pltpu.VMEM((KEPT, HD), BF), pltpu.VMEM((KEPT, HD), F32)
    result = pltpu.VMEM((PAD, HD), F32)
    place = pltpu.VMEM((KEPT, HD), jnp.int32)
    hot = pltpu.VMEM((KEPT, WIDE), BF)
    square_f, square_b = pltpu.VMEM((KEPT, KEPT), F32), pltpu.VMEM((KEPT, KEPT), BF)
    turned = pltpu.VMEM((HD, KEPT), BF)
    dma = pltpu.SemaphoreType.DMA
    out = jax.ShapeDtypeStruct((DEV, TS, HD), BF)
    gain_shape = jax.ShapeDtypeStruct((2, HD), F32)
    merged, gain = pl.pallas_call(
        kernel,
        out_shape=[pltpu.VMEM((4, DEV, TS, HD), BF), pltpu.VMEM((2, HD), F32)],
        in_specs=[hbm] * 7,
        out_specs=[vmem, vmem],
        scratch_shapes=[pltpu.VMEM((2, HD), F32), pltpu.VMEM((2, DEV, TS), jnp.int32)]
        + [pltpu.VMEM((2, DEV), jnp.int32), pltpu.SMEM((2, DEV), jnp.int32)]
        + [pltpu.VMEM((4, DEV, TS, HD), BF)]
        + [message] * 8
        + [pltpu.VMEM((2, MSG, TS), BF)] * 2
        + [pltpu.VMEM((2, 2 * TS, MSG), BF)]
        + [hot] * 2
        + [place] * 2
        + [square_f, square_b, square_b]
        + [rows_b] * 4
        + [rows_f] * 4
        + [turned] * 2
        + [result] * 4
        + [pltpu.VMEM((8, HD), F32), pltpu.VMEM((DEV, 8, HD), F32)]
        + [pltpu.VMEM((8, HD), F32), pltpu.VMEM((DP, 8, HD), F32)]
        + [pltpu.VMEM((2, 8, HD), F32)]
        + [pltpu.SMEM((DEV,), jnp.int32)]
        + [pltpu.SemaphoreType.REGULAR] * 2
        + [dma((8,)), dma((3,)), dma((3,)), dma((2,)), dma((2,))]
        + [dma, dma((DEV,)), dma((3,)), dma((3,))],
        compiler_params=pltpu.CompilerParams(
            collective_id=0, has_side_effects=True, vmem_limit_bytes=60 * 1024 * 1024
        ),
    )(gains, keep_order, keep_count, *pairs)
    results = pl.pallas_call(
        deal,
        out_shape=[out] * 4 + [gain_shape],
        in_specs=[vmem, vmem],
        out_specs=[hbm] * 4 + [vmem],
        scratch_shapes=[dma((4, 4))],
        compiler_params=pltpu.CompilerParams(vmem_limit_bytes=8 * 1024 * 1024),
    )(merged, gain)
    shape = queries.shape
    return tuple(r.reshape(shape) for r in results[:4]) + (results[4],)


def solution(mesh):
    rows = P("dp", None, "ctx", None)
    return jax.shard_map(
        body,
        mesh=mesh,
        in_specs=(rows, rows, rows, rows, P(), P("dp", None, None), P("dp", None)),
        out_specs=(rows, rows, rows, rows, P()),
        check_vma=False,
    )
```
